32 devices in a mesh: groups: 2 (over y), tensor: 4 (over z), dp: 2 (over x), pipe: 2 (over core).
Axes of the slice: x: 2, y: 2, z: 4, core: 2. Of those that a mesh axis runs over, the one named last changes fastest.
Arguments:
- queries: bfloat16 [2048, 8192], P(('groups', 'dp', 'pipe'), 'tensor'), parts along dimension 0, may hold values from -192 to 192
- incoming_key_value: bfloat16 [2048, 2048], P(('groups', 'dp', 'pipe'), 'tensor'), parts along dimension 0, may hold values from -6 to 6
- prefix_key_value_cache: bfloat16 [16, 2048, 2048], P(('groups', 'dp', 'pipe'), None, 'tensor'), parts along dimension 0, may hold values from -6 to 6
- prefix_length: int32 [16], P(('groups', 'dp', 'pipe')), parts along dimension 0, may hold values from 1 to 2048, as said below
- adapter: int32 [16], P(('groups', 'dp', 'pipe')), parts along dimension 0, may hold values from 0 to 3
- output_weight: bfloat16 [8192, 8192], P('tensor', ('dp', 'pipe')), may hold values from -0.0625 to 0.0625
- adapter_down_weight: bfloat16 [8192, 4, 64], P('tensor'), may hold values from -0.0625 to 0.0625
- adapter_up_weight: bfloat16 [4, 64, 8192], P(None, None, 'tensor'), may hold values from -0.75 to 0.75
- residual: bfloat16 [2048, 8192], P(('groups', 'dp', 'pipe'), 'tensor'), parts along dimension 0, may hold values from -1.5 to 1.5
- norm_scale_weight: bfloat16 [8192], P('tensor'), may hold values from 0.5 to 1.5
Outputs:
- hidden: bfloat16 [2048, 8192], P(('groups', 'dp', 'pipe'), 'tensor'), parts along dimension 0
- normed: bfloat16 [2048, 8192], P(('groups', 'dp', 'pipe'), 'tensor'), parts along dimension 0
The draws below stay inside these ranges and needn't reach their ends.
There are 2 independent parts, one for each index of `groups`. The reference program is written for one: setup_inputs(seed, part) draws one part's arguments, and reference() takes and returns one part's arrays. A program takes and returns all parts, laid end to end along the dimension named above; an argument that names none is the same for every part. Nothing has to cross between parts.
Inputs may be any that keep to these rules, and one draw needn't show every extreme that they name: `prefix_length`: some request's prefix fills all 2048 slots.
All inputs are finite; a program needn't handle non-finite values.
Results may differ from the reference program's by a relative error of at most 0.012.
Values may be sent and summed in bfloat16 or wider, within the bound.
A program may use at most 192 MiB of HBM per device.

```python
import math
import jax
import jax.numpy as jnp
import numpy as np
from jax import lax

MODEL_WIDTH = 8192
QUERY_HEADS = 64
HEAD_SIZE = 128
ADAPTER_RANK = 64
ADAPTER_COUNT = 4
NEW = 128
PRE = 2048
KVS = 8
REQUESTS = 8
TOKEN_COUNT = 1024
N_TENSOR = 4


def draw_queries(key, part):
    key = jax.random.fold_in(key, 11)
    values = jnp.clip(jax.random.normal(key, (TOKEN_COUNT, QUERY_HEADS * HEAD_SIZE), jnp.float32), -6.0, 6.0)
    return values.astype(jnp.bfloat16)


def draw_prefix_length(key, part):
    key = jax.random.fold_in(key, 23)
    first_key, second_key = jax.random.split(key)
    lengths = jax.random.randint(first_key, (REQUESTS,), 1, PRE + 1, dtype=jnp.int32)
    fullest = jax.random.randint(second_key, (), 0, REQUESTS, dtype=jnp.int32)
    return jnp.where(jnp.arange(REQUESTS, dtype=jnp.int32) == fullest, jnp.int32(PRE), lengths).astype(jnp.int32)


def place_ends(drawn, key, smallest, top_value):
    longest = drawn.shape.index(max(drawn.shape))
    spots = []
    for shift in (0, 1):
        where = [jax.random.randint(jax.random.fold_in(key, axis), (), 0, length) for axis, length in enumerate(drawn.shape)]
        where[longest] = (where[longest] + shift) % drawn.shape[longest]
        spots.append(tuple(where))
    return drawn.at[spots[0]].set(smallest).at[spots[1]].set(top_value)


def shard_levels(rng, extent, cuts, least, top_value):
    def one(position, parts):
        steps = jax.random.uniform(jax.random.fold_in(jax.random.fold_in(rng, 6), position), (parts,), jnp.float32, least / len(cuts), top_value / len(cuts))
        return jnp.repeat(jnp.exp(steps), extent[position] // parts).reshape((-1,) + (1,) * (len(extent) - position - 1))

    level = one(*cuts[0])
    for cut in cuts[1:]:
        level = level * one(*cut)
    return level


def rank_bounds(number_of, skew):
    portions = [(1 << 20) // math.isqrt(standing ** skew) + 1 for standing in range(1, number_of + 1)]
    spread = 1 + sum(portions) // (1 << 30)
    return np.cumsum(np.array([max(1, weight // spread) for weight in portions]))


def ranked_ids(own_key, dims, number_of, skew):
    grid = rank_bounds(number_of, skew)
    ticket = jax.random.randint(jax.random.fold_in(own_key, 1), dims, 0, int(grid[number_of - 1]))
    grade = jnp.searchsorted(jnp.asarray(grid, jnp.int32), ticket, side="right")
    return jax.random.permutation(jax.random.fold_in(own_key, 2), number_of)[grade].astype(jnp.int32)


def scatter_about(rng, shape, scale, most, cuts=(), held_as=jnp.bfloat16):
    entries = jax.random.normal(rng, shape, jnp.float32) * scale
    if len(cuts) > 0:
        entries = shard_levels(rng, shape, cuts, -0.22, 0.18) * entries
    return jnp.clip(entries, min=-most, max=most).astype(held_as)


def setup_inputs(seed: int = 0, part: int = 0) -> dict:
    keys = jax.random.split(jax.random.key(seed), 11)
    part_keys = jax.random.split(jax.random.fold_in(keys[10], part), 11)
    return {
        "queries": draw_queries(jax.random.fold_in(jax.random.fold_in(keys[10], part), 71), part),
        "incoming_key_value": scatter_about(part_keys[1], (TOKEN_COUNT, KVS * 2 * HEAD_SIZE), 1.0, 6.0, ((0, 4), (1, 4))),
        "prefix_key_value_cache": scatter_about(part_keys[2], (REQUESTS, PRE, KVS * 2 * HEAD_SIZE), 1.0, 6.0, ((0, 4), (2, 4))),
        "prefix_length": draw_prefix_length(jax.random.fold_in(jax.random.fold_in(keys[10], part), 71), part),
        "adapter": place_ends(ranked_ids(part_keys[4], (REQUESTS,), ADAPTER_COUNT, 2), jax.random.fold_in(part_keys[4], 3), 0, ADAPTER_COUNT - 1).astype(jnp.int32),
        "output_weight": scatter_about(keys[5], (QUERY_HEADS * HEAD_SIZE, MODEL_WIDTH), (QUERY_HEADS * HEAD_SIZE) ** -0.5, 0.0625, ((0, 4), (1, 4))),
        "adapter_down_weight": scatter_about(keys[6], (QUERY_HEADS * HEAD_SIZE, ADAPTER_COUNT, ADAPTER_RANK), (QUERY_HEADS * HEAD_SIZE) ** -0.5, 0.0625, ((0, 4),)),
        "adapter_up_weight": scatter_about(keys[7], (ADAPTER_COUNT, ADAPTER_RANK, MODEL_WIDTH), ADAPTER_RANK ** -0.5, 0.75, ((2, 4),)),
        "residual": scatter_about(part_keys[8], (TOKEN_COUNT, MODEL_WIDTH), 0.25, 1.5, ((0, 4), (1, 4))),
        "norm_scale_weight": jnp.clip(1.0 + 0.1 * jax.random.normal(keys[9], (MODEL_WIDTH,), jnp.float32), 0.5, 1.5).astype(jnp.bfloat16),
    }


neg_large = -1e+30
eps_norm = 1e-05

def reorder_heads(packed, rows):
    pair_blocks = N_TENSOR // 2
    block_heads = 2 * KVS // N_TENSOR
    shaped = packed.reshape(REQUESTS, rows, pair_blocks, 2, block_heads, HEAD_SIZE)
    return jnp.transpose(shaped, (0, 1, 2, 4, 3, 5)).reshape(REQUESTS, rows, KVS, 2, HEAD_SIZE)

def reference(queries, incoming_key_value, prefix_key_value_cache, prefix_length, adapter, output_weight, adapter_down_weight, adapter_up_weight, residual, norm_scale_weight):
    grouped = QUERY_HEADS // KVS
    scaling = 1.0 / math.sqrt(HEAD_SIZE)
    query_view = queries.reshape(REQUESTS, NEW, KVS, grouped, HEAD_SIZE)
    fresh_kv = reorder_heads(incoming_key_value, NEW)
    past_kv = reorder_heads(prefix_key_value_cache, PRE)

    def one_request(inputs):
        query_one, fresh_one, past_one, length = inputs
        keys_all = jnp.concatenate([past_one[:, :, 0, :], fresh_one[:, :, 0, :]], axis=0).astype(jnp.float32)
        values_all = jnp.concatenate([past_one[:, :, 1, :], fresh_one[:, :, 1, :]], axis=0).astype(jnp.float32)
        scores = jnp.einsum('nsgd,ksd->nsgk', query_one.astype(jnp.float32), keys_all, precision=lax.Precision.HIGHEST) * scaling
        key_pos = jnp.arange(PRE + NEW)
        token_pos = jnp.arange(NEW)
        visible = jnp.where(key_pos[None, :] < PRE, key_pos[None, :] < length, key_pos[None, :] - PRE <= token_pos[:, None])
        scores = jnp.where(visible[:, None, None, :], scores, neg_large)
        peak = lax.optimization_barrier(jnp.max(scores, axis=-1, keepdims=True))
        weights = jnp.exp(scores - peak)
        denominator = lax.optimization_barrier(jnp.sum(weights, axis=-1))
        rounded = lax.optimization_barrier(weights.astype(jnp.bfloat16)).astype(jnp.float32)
        mixed = jnp.einsum('nsgk,ksd->nsgd', rounded, values_all, precision=lax.Precision.HIGHEST)
        return (mixed / denominator[..., None]).astype(jnp.bfloat16)
    attention_output = lax.map(one_request, (query_view, fresh_kv, past_kv, prefix_length)).reshape(TOKEN_COUNT, QUERY_HEADS * HEAD_SIZE)
    rows_block = QUERY_HEADS * HEAD_SIZE // N_TENSOR
    projected_output = jnp.zeros((TOKEN_COUNT, MODEL_WIDTH), jnp.float32)
    for block_index in range(N_TENSOR):
        lower = block_index * rows_block
        block_term = jnp.dot(attention_output[:, lower:lower + rows_block], output_weight[lower:lower + rows_block], preferred_element_type=jnp.float32)
        block_term = lax.optimization_barrier(block_term.astype(jnp.bfloat16)).astype(jnp.float32)
        projected_output = projected_output + block_term
    adapter_rows = jnp.repeat(adapter, NEW)
    selector = (adapter_rows[:, None] == jnp.arange(ADAPTER_COUNT)[None, :].astype(jnp.int32)).astype(jnp.float32)
    flattened_rank = jnp.dot(attention_output, adapter_down_weight.reshape(QUERY_HEADS * HEAD_SIZE, ADAPTER_COUNT * ADAPTER_RANK), preferred_element_type=jnp.float32).reshape(TOKEN_COUNT, ADAPTER_COUNT, ADAPTER_RANK)
    rank_total = lax.optimization_barrier(jnp.sum(flattened_rank * selector[:, :, None], axis=1))
    shrunk = rank_total.astype(jnp.bfloat16)
    spread_heads = (shrunk[:, None, :] * selector.astype(jnp.bfloat16)[:, :, None]).reshape(TOKEN_COUNT, ADAPTER_COUNT * ADAPTER_RANK)
    adapter_output = jnp.dot(spread_heads, adapter_up_weight.reshape(ADAPTER_COUNT * ADAPTER_RANK, MODEL_WIDTH), preferred_element_type=jnp.float32)
    combined_output = residual.astype(jnp.float32) + projected_output + adapter_output
    hidden = combined_output.astype(jnp.bfloat16)
    widened = hidden.astype(jnp.float32)
    inverse = lax.rsqrt(lax.optimization_barrier(jnp.sum(widened * widened, axis=1)) / MODEL_WIDTH + eps_norm)
    normed = (widened * inverse[:, None] * norm_scale_weight.astype(jnp.float32)[None, :]).astype(jnp.bfloat16)
    return (hidden, normed)
```

```python
import functools
import math

import jax
import jax.numpy as jnp
from jax import lax
from jax.experimental import pallas as pl
from jax.experimental.pallas import tpu as pltpu
from jax.sharding import PartitionSpec as P

MODEL_WIDTH = 8192
HEAD_SIZE = 128
ADAPTER_RANK = 64
ADAPTER_COUNT = 4
NEW = 128
PRE = 2048


neg_large = -1e30
eps_norm = 1e-05


def partner(block, axis, distance):
    count = lax.axis_size(axis)
    route = []
    for low in range(count):
        high = low | 1 << distance
        if high != low and high < count:
            route += [(low, high), (high, low)]
    return lax.ppermute(block, axis, route)


def shards_any(
    queries,
    incoming_key_value,
    prefix_key_value_cache,
    prefix_length,
    adapter,
    output_weight,
    adapter_down_weight,
    adapter_up_weight,
    residual,
    norm_scale_weight,
):
    requests = prefix_length.shape[0]
    tokens = queries.shape[0]
    heads_dev = queries.shape[1] // HEAD_SIZE
    block_heads = incoming_key_value.shape[1] // HEAD_SIZE
    scaling = 1.0 / math.sqrt(HEAD_SIZE)
    partner_new, partner_past = partner((incoming_key_value, prefix_key_value_cache), "tensor", 0)
    parity = lax.axis_index("tensor") % 2
    holds_keys = parity == 0
    fresh_keys = jnp.where(holds_keys, incoming_key_value, partner_new).reshape(
        requests, NEW, block_heads, HEAD_SIZE
    )
    fresh_values = jnp.where(holds_keys, partner_new, incoming_key_value).reshape(
        requests, NEW, block_heads, HEAD_SIZE
    )
    past_keys = jnp.where(holds_keys, prefix_key_value_cache, partner_past).reshape(
        requests, PRE, block_heads, HEAD_SIZE
    )
    past_values = jnp.where(holds_keys, partner_past, prefix_key_value_cache).reshape(
        requests, PRE, block_heads, HEAD_SIZE
    )
    slots_dev = max(1, block_heads // 2)
    offset = parity * (block_heads - slots_dev)
    fresh_kv = jnp.stack(
        [
            lax.dynamic_slice_in_dim(fresh_keys, offset, slots_dev, 2),
            lax.dynamic_slice_in_dim(fresh_values, offset, slots_dev, 2),
        ],
        axis=3,
    )
    past_kv = jnp.stack(
        [
            lax.dynamic_slice_in_dim(past_keys, offset, slots_dev, 2),
            lax.dynamic_slice_in_dim(past_values, offset, slots_dev, 2),
        ],
        axis=3,
    )
    grouped = heads_dev // slots_dev
    query_view = queries.reshape(requests, NEW, slots_dev, grouped, HEAD_SIZE)
    scores = (
        jnp.einsum(
            "rnsgd,rksd->rnsgk",
            query_view,
            fresh_kv[:, :, :, 0, :],
            preferred_element_type=jnp.float32,
        )
        * scaling
    )
    causal = jnp.arange(NEW)[None, :] <= jnp.arange(NEW)[:, None]
    scores = jnp.where(causal[None, :, None, None, :], scores, neg_large)
    running_max = jnp.max(scores, axis=-1)
    weights = jnp.exp(scores - running_max[..., None])
    denominator = jnp.sum(weights, axis=-1)
    weighted = jnp.einsum(
        "rnsgk,rksd->rnsgd",
        weights.astype(jnp.bfloat16),
        fresh_kv[:, :, :, 1, :],
        preferred_element_type=jnp.float32,
    )
    key_width = min(PRE, 512)

    def key_step(block_index, state_carry):
        old_max, old_denominator, old_weighted = state_carry
        key_block = lax.dynamic_slice_in_dim(past_kv, block_index * key_width, key_width, 1)
        block_scores = (
            jnp.einsum(
                "rnsgd,rksd->rnsgk",
                query_view,
                key_block[:, :, :, 0, :],
                preferred_element_type=jnp.float32,
            )
            * scaling
        )
        position = block_index * key_width + jnp.arange(key_width)
        live_mask = position[None, :] < prefix_length[:, None]
        block_scores = jnp.where(live_mask[:, None, None, None, :], block_scores, neg_large)
        new_max = jnp.maximum(old_max, jnp.max(block_scores, axis=-1))
        shrink = jnp.exp(old_max - new_max)
        block_weights = jnp.exp(block_scores - new_max[..., None])
        new_denominator = old_denominator * shrink + jnp.sum(block_weights, axis=-1)
        new_weighted = old_weighted * shrink[..., None] + jnp.einsum(
            "rnsgk,rksd->rnsgd",
            block_weights.astype(jnp.bfloat16),
            key_block[:, :, :, 1, :],
            preferred_element_type=jnp.float32,
        )
        return (new_max, new_denominator, new_weighted)

    block_count = PRE // key_width
    running_max, denominator, weighted = lax.fori_loop(
        0, block_count, key_step, (running_max, denominator, weighted)
    )
    attention_output = (
        (weighted / denominator[..., None])
        .astype(jnp.bfloat16)
        .reshape(tokens, heads_dev * HEAD_SIZE)
    )
    partial_value = jnp.dot(
        attention_output,
        lax.all_gather(output_weight, ("dp", "pipe"), axis=1, tiled=True),
        preferred_element_type=jnp.float32,
    )
    projected_output = lax.psum_scatter(
        partial_value.astype(jnp.bfloat16), "tensor", scatter_dimension=1, tiled=True
    ).astype(jnp.float32)
    adapter_rows = jnp.repeat(adapter, NEW)
    selector = (adapter_rows[:, None] == jnp.arange(ADAPTER_COUNT)[None, :]).astype(jnp.float32)
    flattened_rank = jnp.dot(
        attention_output,
        adapter_down_weight.reshape(adapter_down_weight.shape[0], ADAPTER_COUNT * ADAPTER_RANK),
        preferred_element_type=jnp.float32,
    ).reshape(tokens, ADAPTER_COUNT, ADAPTER_RANK)
    partial_rank = jnp.sum(flattened_rank * selector[:, :, None], axis=1)
    pieces = lax.all_gather(partial_rank.astype(jnp.bfloat16), "tensor", axis=1, tiled=True).astype(
        partial_rank.dtype
    )
    rank_total = jnp.sum(pieces.reshape(tokens, -1, ADAPTER_RANK), axis=1)
    shrunk = rank_total.astype(jnp.bfloat16)
    spread_heads = (shrunk[:, None, :] * selector.astype(jnp.bfloat16)[:, :, None]).reshape(
        tokens, ADAPTER_COUNT * ADAPTER_RANK
    )
    adapter_output = jnp.dot(
        spread_heads,
        adapter_up_weight.reshape(ADAPTER_COUNT * ADAPTER_RANK, adapter_up_weight.shape[2]),
        preferred_element_type=jnp.float32,
    )
    combined_output = residual.astype(jnp.float32) + projected_output + adapter_output
    hidden = combined_output.astype(jnp.bfloat16)
    widened = hidden.astype(jnp.float32)
    squares = lax.psum(jnp.sum(widened * widened, axis=1), "tensor")
    inverse = lax.rsqrt(squares / MODEL_WIDTH + eps_norm)
    normed = (widened * inverse[:, None] * norm_scale_weight.astype(jnp.float32)[None, :]).astype(
        jnp.bfloat16
    )
    return (hidden, normed)


def attend_kernel(
    heads_tile, length_ref, parity_ref, q_ref, own_past, own_new, recv, out_ref, keys, values
):
    request = pl.program_id(0)
    row_tile = 2
    past, new = own_past.shape[1], own_new.shape[0]

    @pl.when((pl.program_id(2) == 0) & (parity_ref[0] == 0))
    def _():
        keys[:past] = own_past[0]
        keys[past:] = own_new[...]
        values[...] = recv[...]

    @pl.when((pl.program_id(2) == 0) & (parity_ref[0] != 0))
    def _():
        values[:past] = own_past[0]
        values[past:] = own_new[...]
        keys[...] = recv[...]

    factor = math.log2(math.e) / math.sqrt(HEAD_SIZE)
    length = length_ref[request + parity_ref[1]]
    live = lax.broadcasted_iota(jnp.int32, (1, past), 1) < length
    bias = jnp.where(live, 0.0, neg_large)
    rows = row_tile * new
    row = lax.broadcasted_iota(jnp.int32, (rows, new), 0) % new
    causal = lax.broadcasted_iota(jnp.int32, (rows, new), 1) <= row
    for first in range(0, heads_tile, row_tile):
        q = jnp.concatenate(
            [
                q_ref[:, h * HEAD_SIZE : (h + 1) * HEAD_SIZE]
                for h in range(first, first + row_tile)
            ],
            axis=0,
        )
        scores = lax.dot_general(
            q, keys[...], (((1,), (1,)), ((), ())), preferred_element_type=jnp.float32
        )
        old = scores[:, :past] + bias
        fresh = jnp.where(causal, scores[:, past:], neg_large)
        peak = jnp.maximum(
            jnp.max(old, axis=1, keepdims=True), jnp.max(fresh, axis=1, keepdims=True)
        )
        old = jnp.exp2((old - peak) * factor)
        fresh = jnp.exp2((fresh - peak) * factor)
        denominator = jnp.sum(old, axis=1, keepdims=True) + jnp.sum(fresh, axis=1, keepdims=True)
        mixed = jnp.dot(
            old.astype(jnp.bfloat16), values[:past], preferred_element_type=jnp.float32
        ) + jnp.dot(
            fresh.astype(jnp.bfloat16), values[past:], preferred_element_type=jnp.float32
        )
        mixed = (mixed / denominator).astype(jnp.bfloat16)
        for i in range(row_tile):
            h = first + i
            out_ref[:, h * HEAD_SIZE : (h + 1) * HEAD_SIZE] = mixed[i * new : (i + 1) * new]


def attend(request, lengths, parity, queries, cache, incoming, recv):
    slots = recv.shape[1] // HEAD_SIZE
    heads = queries.shape[1] // HEAD_SIZE
    grouped = heads // slots
    heads_tile = min(4, grouped)
    tiles = grouped // heads_tile
    past = cache.shape[1]
    whole = past + NEW
    meta = jnp.stack([parity, jnp.int32(request)])
    width = heads_tile * HEAD_SIZE
    return pl.pallas_call(
        functools.partial(attend_kernel, heads_tile),
        out_shape=jax.ShapeDtypeStruct((NEW, heads * HEAD_SIZE), jnp.bfloat16),
        grid_spec=pltpu.PrefetchScalarGridSpec(
            num_scalar_prefetch=2,
            grid=(1, slots, tiles),
            in_specs=[
                pl.BlockSpec((NEW, width), lambda r, s, t, n, p: (request, s * tiles + t)),
                pl.BlockSpec(
                    (1, past, HEAD_SIZE), lambda r, s, t, n, p: (request, 0, slots * p[0] + s)
                ),
                pl.BlockSpec((NEW, HEAD_SIZE), lambda r, s, t, n, p: (request, slots * p[0] + s)),
                pl.BlockSpec((whole, HEAD_SIZE), lambda r, s, t, n, p: (0, s)),
            ],
            out_specs=pl.BlockSpec((NEW, width), lambda r, s, t, n, p: (0, s * tiles + t)),
            scratch_shapes=[
                pltpu.VMEM((whole, HEAD_SIZE), jnp.bfloat16),
                pltpu.VMEM((whole, HEAD_SIZE), jnp.bfloat16),
            ],
        ),
        compiler_params=pltpu.CompilerParams(vmem_limit_bytes=40 * 2**20),
        cost_estimate=pl.CostEstimate(
            flops=4 * NEW * heads * whole * HEAD_SIZE,
            bytes_accessed=4 * whole * slots * HEAD_SIZE + 4 * NEW * heads * HEAD_SIZE,
            transcendentals=NEW * heads * whole,
        ),
        name="attend",
    )(lengths, meta, queries, cache, incoming, recv)


def from_others(block, axis):
    count = lax.axis_size(axis)
    return [
        lax.ppermute(block, axis, [(i, (i + shift) % count) for i in range(count)])
        for shift in range(1, count)
    ]


def shards_fast(
    queries,
    incoming_key_value,
    prefix_key_value_cache,
    prefix_length,
    adapter,
    output_weight,
    adapter_down_weight,
    adapter_up_weight,
    residual,
    norm_scale_weight,
):
    requests = prefix_length.shape[0]
    half = incoming_key_value.shape[1] // 2
    past = prefix_key_value_cache.shape[1]
    width = output_weight.shape[1]
    place = lax.axis_index("tensor")
    parity = place % 2
    upper = place // 2
    x = lax.axis_index("dp")
    core = lax.axis_index("pipe")
    send_at = (1 - parity) * half
    outgoing = []
    for r in range(requests):
        a = lax.dynamic_slice(prefix_key_value_cache, (r, 0, send_at), (1, past, half))[0]
        b = lax.dynamic_slice(incoming_key_value, (r * NEW, send_at), (NEW, half))
        outgoing.append(jnp.concatenate([a, b], axis=0))
    arrived = [partner(block, "tensor", 0) for block in outgoing]
    weight_partner = partner(output_weight, "pipe", 0)
    down = adapter_down_weight.reshape(adapter_down_weight.shape[0], ADAPTER_COUNT * ADAPTER_RANK)

    keep_own = parity == core
    hidden, squares = [], []
    for r in range(requests):
        attended = attend(
            r, prefix_length, parity, queries, prefix_key_value_cache, incoming_key_value, arrived[r]
        )
        both = jnp.concatenate([attended, partner(attended, "dp", 0)], axis=0)
        own = jnp.dot(both, output_weight, preferred_element_type=jnp.float32).astype(jnp.bfloat16)
        other = jnp.dot(both, weight_partner, preferred_element_type=jnp.float32).astype(
            jnp.bfloat16
        )
        kept = jnp.where(keep_own, own, other)
        sent = jnp.where(keep_own, other, own)
        got = partner(sent, "tensor", 0)
        pair = (kept.astype(jnp.float32) + got.astype(jnp.float32)).astype(jnp.bfloat16)
        mine = pair[:NEW]
        theirs = partner(pair[NEW:], "dp", 0)
        last_kept = jnp.where(x == upper, mine, theirs)
        last_sent = jnp.where(x == upper, theirs, mine)
        last_got = partner(last_sent, "tensor", 1)
        projected = last_kept.astype(jnp.float32) + last_got.astype(jnp.float32)

        flat = jnp.dot(attended, down, preferred_element_type=jnp.float32)
        partial = lax.dynamic_slice(flat, (0, adapter[r] * ADAPTER_RANK), (NEW, ADAPTER_RANK))
        partial = partial.astype(jnp.bfloat16)
        rank_total = partial.astype(jnp.float32)
        for piece in from_others(partial, "tensor"):
            rank_total = rank_total + piece.astype(jnp.float32)
        up = lax.dynamic_slice(
            adapter_up_weight, (adapter[r], 0, 0), (1, ADAPTER_RANK, width)
        )[0]
        adapter_output = jnp.dot(
            rank_total.astype(jnp.bfloat16), up, preferred_element_type=jnp.float32
        )
        rows = residual[r * NEW : (r + 1) * NEW].astype(jnp.float32)
        hidden.append((rows + projected + adapter_output).astype(jnp.bfloat16))
    hidden = jnp.concatenate(hidden, axis=0)
    widened = hidden.astype(jnp.float32)
    own_squares = jnp.sum(widened * widened, axis=1)
    squares = own_squares
    for piece in from_others(own_squares, "tensor"):
        squares = squares + piece
    inverse = lax.rsqrt(squares / MODEL_WIDTH + eps_norm)
    normed = (widened * inverse[:, None] * norm_scale_weight.astype(jnp.float32)[None, :]).astype(
        jnp.bfloat16
    )
    return (hidden, normed)


def solution(mesh):
    sizes = tuple(mesh.shape[name] for name in ("tensor", "dp", "pipe"))
    shards = shards_fast if sizes == (4, 2, 2) else shards_any
    return jax.shard_map(
        shards,
        mesh=mesh,
        in_specs=(
            P(("groups", "dp", "pipe"), "tensor"),
            P(("groups", "dp", "pipe"), "tensor"),
            P(("groups", "dp", "pipe"), None, "tensor"),
            P(("groups", "dp", "pipe")),
            P(("groups", "dp", "pipe")),
            P("tensor", ("dp", "pipe")),
            P("tensor", None, None),
            P(None, None, "tensor"),
            P(("groups", "dp", "pipe"), "tensor"),
            P("tensor"),
        ),
        out_specs=(P(("groups", "dp", "pipe"), "tensor"), P(("groups", "dp", "pipe"), "tensor")),
        check_vma=False,
    )
```

```python
import functools
import math

import jax
import jax.numpy as jnp
from jax import lax
from jax.experimental import pallas as pl
from jax.experimental.pallas import tpu as pltpu
from jax.sharding import PartitionSpec as P

MODEL_WIDTH = 8192
HEAD_SIZE = 128
ADAPTER_RANK = 64
ADAPTER_COUNT = 4
NEW = 128
PRE = 2048


neg_large = -1e30
eps_norm = 1e-05


def partner(block, axis, distance):
    count = lax.axis_size(axis)
    route = []
    for low in range(count):
        high = low | 1 << distance
        if high != low and high < count:
            route += [(low, high), (high, low)]
    return lax.ppermute(block, axis, route)


def shards_any(
    queries,
    incoming_key_value,
    prefix_key_value_cache,
    prefix_length,
    adapter,
    output_weight,
    adapter_down_weight,
    adapter_up_weight,
    residual,
    norm_scale_weight,
):
    requests = prefix_length.shape[0]
    tokens = queries.shape[0]
    heads_dev = queries.shape[1] // HEAD_SIZE
    block_heads = incoming_key_value.shape[1] // HEAD_SIZE
    scaling = 1.0 / math.sqrt(HEAD_SIZE)
    partner_new, partner_past = partner((incoming_key_value, prefix_key_value_cache), "tensor", 0)
    parity = lax.axis_index("tensor") % 2
    holds_keys = parity == 0
    fresh_keys = jnp.where(holds_keys, incoming_key_value, partner_new).reshape(
        requests, NEW, block_heads, HEAD_SIZE
    )
    fresh_values = jnp.where(holds_keys, partner_new, incoming_key_value).reshape(
        requests, NEW, block_heads, HEAD_SIZE
    )
    past_keys = jnp.where(holds_keys, prefix_key_value_cache, partner_past).reshape(
        requests, PRE, block_heads, HEAD_SIZE
    )
    past_values = jnp.where(holds_keys, partner_past, prefix_key_value_cache).reshape(
        requests, PRE, block_heads, HEAD_SIZE
    )
    slots_dev = max(1, block_heads // 2)
    offset = parity * (block_heads - slots_dev)
    fresh_kv = jnp.stack(
        [
            lax.dynamic_slice_in_dim(fresh_keys, offset, slots_dev, 2),
            lax.dynamic_slice_in_dim(fresh_values, offset, slots_dev, 2),
        ],
        axis=3,
    )
    past_kv = jnp.stack(
        [
            lax.dynamic_slice_in_dim(past_keys, offset, slots_dev, 2),
            lax.dynamic_slice_in_dim(past_values, offset, slots_dev, 2),
        ],
        axis=3,
    )
    grouped = heads_dev // slots_dev
    query_view = queries.reshape(requests, NEW, slots_dev, grouped, HEAD_SIZE)
    scores = (
        jnp.einsum(
            "rnsgd,rksd->rnsgk",
            query_view,
            fresh_kv[:, :, :, 0, :],
            preferred_element_type=jnp.float32,
        )
        * scaling
    )
    causal = jnp.arange(NEW)[None, :] <= jnp.arange(NEW)[:, None]
    scores = jnp.where(causal[None, :, None, None, :], scores, neg_large)
    running_max = jnp.max(scores, axis=-1)
    weights = jnp.exp(scores - running_max[..., None])
    denominator = jnp.sum(weights, axis=-1)
    weighted = jnp.einsum(
        "rnsgk,rksd->rnsgd",
        weights.astype(jnp.bfloat16),
        fresh_kv[:, :, :, 1, :],
        preferred_element_type=jnp.float32,
    )
    key_width = min(PRE, 512)

    def key_step(block_index, state_carry):
        old_max, old_denominator, old_weighted = state_carry
        key_block = lax.dynamic_slice_in_dim(past_kv, block_index * key_width, key_width, 1)
        block_scores = (
            jnp.einsum(
                "rnsgd,rksd->rnsgk",
                query_view,
                key_block[:, :, :, 0, :],
                preferred_element_type=jnp.float32,
            )
            * scaling
        )
        position = block_index * key_width + jnp.arange(key_width)
        live_mask = position[None, :] < prefix_length[:, None]
        block_scores = jnp.where(live_mask[:, None, None, None, :], block_scores, neg_large)
        new_max = jnp.maximum(old_max, jnp.max(block_scores, axis=-1))
        shrink = jnp.exp(old_max - new_max)
        block_weights = jnp.exp(block_scores - new_max[..., None])
        new_denominator = old_denominator * shrink + jnp.sum(block_weights, axis=-1)
        new_weighted = old_weighted * shrink[..., None] + jnp.einsum(
            "rnsgk,rksd->rnsgd",
            block_weights.astype(jnp.bfloat16),
            key_block[:, :, :, 1, :],
            preferred_element_type=jnp.float32,
        )
        return (new_max, new_denominator, new_weighted)

    block_count = PRE // key_width
    running_max, denominator, weighted = lax.fori_loop(
        0, block_count, key_step, (running_max, denominator, weighted)
    )
    attention_output = (
        (weighted / denominator[..., None])
        .astype(jnp.bfloat16)
        .reshape(tokens, heads_dev * HEAD_SIZE)
    )
    partial_value = jnp.dot(
        attention_output,
        lax.all_gather(output_weight, ("dp", "pipe"), axis=1, tiled=True),
        preferred_element_type=jnp.float32,
    )
    projected_output = lax.psum_scatter(
        partial_value.astype(jnp.bfloat16), "tensor", scatter_dimension=1, tiled=True
    ).astype(jnp.float32)
    adapter_rows = jnp.repeat(adapter, NEW)
    selector = (adapter_rows[:, None] == jnp.arange(ADAPTER_COUNT)[None, :]).astype(jnp.float32)
    flattened_rank = jnp.dot(
        attention_output,
        adapter_down_weight.reshape(adapter_down_weight.shape[0], ADAPTER_COUNT * ADAPTER_RANK),
        preferred_element_type=jnp.float32,
    ).reshape(tokens, ADAPTER_COUNT, ADAPTER_RANK)
    partial_rank = jnp.sum(flattened_rank * selector[:, :, None], axis=1)
    pieces = lax.all_gather(partial_rank.astype(jnp.bfloat16), "tensor", axis=1, tiled=True).astype(
        partial_rank.dtype
    )
    rank_total = jnp.sum(pieces.reshape(tokens, -1, ADAPTER_RANK), axis=1)
    shrunk = rank_total.astype(jnp.bfloat16)
    spread_heads = (shrunk[:, None, :] * selector.astype(jnp.bfloat16)[:, :, None]).reshape(
        tokens, ADAPTER_COUNT * ADAPTER_RANK
    )
    adapter_output = jnp.dot(
        spread_heads,
        adapter_up_weight.reshape(ADAPTER_COUNT * ADAPTER_RANK, adapter_up_weight.shape[2]),
        preferred_element_type=jnp.float32,
    )
    combined_output = residual.astype(jnp.float32) + projected_output + adapter_output
    hidden = combined_output.astype(jnp.bfloat16)
    widened = hidden.astype(jnp.float32)
    squares = lax.psum(jnp.sum(widened * widened, axis=1), "tensor")
    inverse = lax.rsqrt(squares / MODEL_WIDTH + eps_norm)
    normed = (widened * inverse[:, None] * norm_scale_weight.astype(jnp.float32)[None, :]).astype(
        jnp.bfloat16
    )
    return (hidden, normed)


def attend_kernel(
    heads_tile, length_ref, parity_ref, q_ref, own_past, own_new, recv, out_ref, keys, values
):
    request = pl.program_id(0)
    row_tile = 2
    past, new = own_past.shape[1], own_new.shape[0]

    @pl.when((pl.program_id(2) == 0) & (parity_ref[0] == 0))
    def _():
        keys[:past] = own_past[0]
        keys[past:] = own_new[...]
        values[...] = recv[...]

    @pl.when((pl.program_id(2) == 0) & (parity_ref[0] != 0))
    def _():
        values[:past] = own_past[0]
        values[past:] = own_new[...]
        keys[...] = recv[...]

    factor = math.log2(math.e) / math.sqrt(HEAD_SIZE)
    length = length_ref[request + parity_ref[1]]
    live = lax.broadcasted_iota(jnp.int32, (1, past), 1) < length
    bias = jnp.where(live, 0.0, neg_large)
    rows = row_tile * new
    row = lax.broadcasted_iota(jnp.int32, (rows, new), 0) % new
    causal = lax.broadcasted_iota(jnp.int32, (rows, new), 1) <= row
    for first in range(0, heads_tile, row_tile):
        q = jnp.concatenate(
            [
                q_ref[:, h * HEAD_SIZE : (h + 1) * HEAD_SIZE]
                for h in range(first, first + row_tile)
            ],
            axis=0,
        )
        scores = lax.dot_general(
            q, keys[...], (((1,), (1,)), ((), ())), preferred_element_type=jnp.float32
        )
        old = scores[:, :past] + bias
        fresh = jnp.where(causal, scores[:, past:], neg_large)
        peak = jnp.maximum(
            jnp.max(old, axis=1, keepdims=True), jnp.max(fresh, axis=1, keepdims=True)
        )
        old = jnp.exp2((old - peak) * factor)
        fresh = jnp.exp2((fresh - peak) * factor)
        denominator = jnp.sum(old, axis=1, keepdims=True) + jnp.sum(fresh, axis=1, keepdims=True)
        mixed = jnp.dot(
            old.astype(jnp.bfloat16), values[:past], preferred_element_type=jnp.float32
        ) + jnp.dot(
            fresh.astype(jnp.bfloat16), values[past:], preferred_element_type=jnp.float32
        )
        mixed = (mixed / denominator).astype(jnp.bfloat16)
        for i in range(row_tile):
            h = first + i
            out_ref[:, h * HEAD_SIZE : (h + 1) * HEAD_SIZE] = mixed[i * new : (i + 1) * new]


def attend(request, lengths, parity, queries, cache, incoming, recv):
    slots = recv.shape[1] // HEAD_SIZE
    heads = queries.shape[1] // HEAD_SIZE
    grouped = heads // slots
    heads_tile = min(4, grouped)
    tiles = grouped // heads_tile
    past = cache.shape[1]
    whole = past + NEW
    meta = jnp.stack([parity, jnp.int32(request)])
    width = heads_tile * HEAD_SIZE
    return pl.pallas_call(
        functools.partial(attend_kernel, heads_tile),
        out_shape=jax.ShapeDtypeStruct((NEW, heads * HEAD_SIZE), jnp.bfloat16),
        grid_spec=pltpu.PrefetchScalarGridSpec(
            num_scalar_prefetch=2,
            grid=(1, slots, tiles),
            in_specs=[
                pl.BlockSpec((NEW, width), lambda r, s, t, n, p: (request, s * tiles + t)),
                pl.BlockSpec(
                    (1, past, HEAD_SIZE), lambda r, s, t, n, p: (request, 0, slots * p[0] + s)
                ),
                pl.BlockSpec((NEW, HEAD_SIZE), lambda r, s, t, n, p: (request, slots * p[0] + s)),
                pl.BlockSpec((whole, HEAD_SIZE), lambda r, s, t, n, p: (0, s)),
            ],
            out_specs=pl.BlockSpec((NEW, width), lambda r, s, t, n, p: (0, s * tiles + t)),
            scratch_shapes=[
                pltpu.VMEM((whole, HEAD_SIZE), jnp.bfloat16),
                pltpu.VMEM((whole, HEAD_SIZE), jnp.bfloat16),
            ],
        ),
        compiler_params=pltpu.CompilerParams(vmem_limit_bytes=40 * 2**20),
        cost_estimate=pl.CostEstimate(
            flops=4 * NEW * heads * whole * HEAD_SIZE,
            bytes_accessed=4 * whole * slots * HEAD_SIZE + 4 * NEW * heads * HEAD_SIZE,
            transcendentals=NEW * heads * whole,
        ),
        name="attend",
    )(lengths, meta, queries, cache, incoming, recv)


def from_others(block, axis):
    count = lax.axis_size(axis)
    return [
        lax.ppermute(block, axis, [(i, (i + shift) % count) for i in range(count)])
        for shift in range(1, count)
    ]


def shards_fast(
    queries,
    incoming_key_value,
    prefix_key_value_cache,
    prefix_length,
    adapter,
    output_weight,
    adapter_down_weight,
    adapter_up_weight,
    residual,
    norm_scale_weight,
):
    requests = prefix_length.shape[0]
    half = incoming_key_value.shape[1] // 2
    past = prefix_key_value_cache.shape[1]
    width = output_weight.shape[1]
    place = lax.axis_index("tensor")
    parity = place % 2
    upper = place // 2
    x = lax.axis_index("dp")
    core = lax.axis_index("pipe")
    send_at = (1 - parity) * half
    outgoing = []
    for r in range(requests):
        a = lax.dynamic_slice(prefix_key_value_cache, (r, 0, send_at), (1, past, half))[0]
        b = lax.dynamic_slice(incoming_key_value, (r * NEW, send_at), (NEW, half))
        outgoing.append(jnp.concatenate([a, b], axis=0))
    arrived = [partner(block, "tensor", 0) for block in outgoing]
    weight_partner = partner(output_weight, "pipe", 0)
    down = adapter_down_weight.reshape(adapter_down_weight.shape[0], ADAPTER_COUNT * ADAPTER_RANK)

    keep_own = parity == core
    weight_keep = jnp.where(keep_own, output_weight, weight_partner)
    weight_send = jnp.where(keep_own, weight_partner, output_weight)
    weight_keep, weight_send, arrived[0] = lax.optimization_barrier(
        (weight_keep, weight_send, arrived[0])
    )

    def product(rows, weight):
        return jnp.dot(rows, weight, preferred_element_type=jnp.float32).astype(jnp.bfloat16)

    state = []
    for r in range(requests):
        attended = attend(
            r, prefix_length, parity, queries, prefix_key_value_cache, incoming_key_value, arrived[r]
        )
        across = partner(attended, "dp", 0)
        flat = jnp.dot(attended, down, preferred_element_type=jnp.float32)
        rank = lax.dynamic_slice(
            flat, (0, adapter[r] * ADAPTER_RANK), (NEW, ADAPTER_RANK)
        ).astype(jnp.bfloat16)
        rank = jnp.pad(rank, ((0, 0), (0, HEAD_SIZE - ADAPTER_RANK)))
        payload = jnp.concatenate([product(attended, weight_send), rank], axis=1)
        got_mine = partner(payload, "tensor", 0)
        keep_mine = product(attended, weight_keep)
        sent_theirs = product(across, weight_send)
        if r + 1 < requests:
            keep_mine, arrived[r + 1], _ = lax.optimization_barrier(
                (keep_mine, arrived[r + 1], sent_theirs)
            )
        got_theirs = partner(sent_theirs, "tensor", 0)
        keep_theirs = product(across, weight_keep)
        keep_mine, keep_theirs = lax.optimization_barrier((keep_mine, keep_theirs))
        state.append((rank, keep_mine, keep_theirs, got_mine, got_theirs))

    hidden = []
    for r in range(requests):
        rank, keep_mine, keep_theirs, got_mine, got_theirs = state[r]
        theirs_pair = (keep_theirs.astype(jnp.float32) + got_theirs.astype(jnp.float32)).astype(
            jnp.bfloat16
        )
        theirs = partner(theirs_pair, "dp", 0)
        mine = (keep_mine.astype(jnp.float32) + got_mine[:, :width].astype(jnp.float32)).astype(
            jnp.bfloat16
        )
        rank_pair = (rank.astype(jnp.float32) + got_mine[:, width:].astype(jnp.float32)).astype(
            jnp.bfloat16
        )
        last_kept = jnp.where(x == upper, mine, theirs)
        last_sent = jnp.concatenate([jnp.where(x == upper, theirs, mine), rank_pair], axis=1)
        last_got = partner(last_sent, "tensor", 1)
        projected = last_kept.astype(jnp.float32) + last_got[:, :width].astype(jnp.float32)
        shrunk = (rank_pair.astype(jnp.float32) + last_got[:, width:].astype(jnp.float32)).astype(
            jnp.bfloat16
        )
        up = lax.dynamic_slice(
            adapter_up_weight, (adapter[r], 0, 0), (1, ADAPTER_RANK, width)
        )[0]
        adapter_output = jnp.dot(shrunk[:, :ADAPTER_RANK], up, preferred_element_type=jnp.float32)
        rows = residual[r * NEW : (r + 1) * NEW].astype(jnp.float32)
        hidden.append((rows + projected + adapter_output).astype(jnp.bfloat16))
    hidden = jnp.concatenate(hidden, axis=0)
    widened = hidden.astype(jnp.float32)
    own_squares = jnp.sum(widened * widened, axis=1)
    squares = own_squares
    for piece in from_others(own_squares, "tensor"):
        squares = squares + piece
    inverse = lax.rsqrt(squares / MODEL_WIDTH + eps_norm)
    normed = (widened * inverse[:, None] * norm_scale_weight.astype(jnp.float32)[None, :]).astype(
        jnp.bfloat16
    )
    return (hidden, normed)


def solution(mesh):
    sizes = tuple(mesh.shape[name] for name in ("tensor", "dp", "pipe"))
    shards = shards_fast if sizes == (4, 2, 2) else shards_any
    return jax.shard_map(
        shards,
        mesh=mesh,
        in_specs=(
            P(("groups", "dp", "pipe"), "tensor"),
            P(("groups", "dp", "pipe"), "tensor"),
            P(("groups", "dp", "pipe"), None, "tensor"),
            P(("groups", "dp", "pipe")),
            P(("groups", "dp", "pipe")),
            P("tensor", ("dp", "pipe")),
            P("tensor", None, None),
            P(None, None, "tensor"),
            P(("groups", "dp", "pipe"), "tensor"),
            P("tensor"),
        ),
        out_specs=(P(("groups", "dp", "pipe"), "tensor"), P(("groups", "dp", "pipe"), "tensor")),
        check_vma=False,
    )
```

```python
import functools
import math

import jax
import jax.numpy as jnp
from jax import lax
from jax.experimental import pallas as pl
from jax.experimental.pallas import tpu as pltpu
from jax.sharding import PartitionSpec as P

MODEL_WIDTH = 8192
HEAD_SIZE = 128
ADAPTER_RANK = 64
ADAPTER_COUNT = 4
NEW = 128
PRE = 2048


neg_large = -1e30
eps_norm = 1e-05


def partner(block, axis, distance):
    count = lax.axis_size(axis)
    route = []
    for low in range(count):
        high = low | 1 << distance
        if high != low and high < count:
            route += [(low, high), (high, low)]
    return lax.ppermute(block, axis, route)


def shards_any(
    queries,
    incoming_key_value,
    prefix_key_value_cache,
    prefix_length,
    adapter,
    output_weight,
    adapter_down_weight,
    adapter_up_weight,
    residual,
    norm_scale_weight,
):
    requests = prefix_length.shape[0]
    tokens = queries.shape[0]
    heads_dev = queries.shape[1] // HEAD_SIZE
    block_heads = incoming_key_value.shape[1] // HEAD_SIZE
    scaling = 1.0 / math.sqrt(HEAD_SIZE)
    partner_new, partner_past = partner((incoming_key_value, prefix_key_value_cache), "tensor", 0)
    parity = lax.axis_index("tensor") % 2
    holds_keys = parity == 0
    fresh_keys = jnp.where(holds_keys, incoming_key_value, partner_new).reshape(
        requests, NEW, block_heads, HEAD_SIZE
    )
    fresh_values = jnp.where(holds_keys, partner_new, incoming_key_value).reshape(
        requests, NEW, block_heads, HEAD_SIZE
    )
    past_keys = jnp.where(holds_keys, prefix_key_value_cache, partner_past).reshape(
        requests, PRE, block_heads, HEAD_SIZE
    )
    past_values = jnp.where(holds_keys, partner_past, prefix_key_value_cache).reshape(
        requests, PRE, block_heads, HEAD_SIZE
    )
    slots_dev = max(1, block_heads // 2)
    offset = parity * (block_heads - slots_dev)
    fresh_kv = jnp.stack(
        [
            lax.dynamic_slice_in_dim(fresh_keys, offset, slots_dev, 2),
            lax.dynamic_slice_in_dim(fresh_values, offset, slots_dev, 2),
        ],
        axis=3,
    )
    past_kv = jnp.stack(
        [
            lax.dynamic_slice_in_dim(past_keys, offset, slots_dev, 2),
            lax.dynamic_slice_in_dim(past_values, offset, slots_dev, 2),
        ],
        axis=3,
    )
    grouped = heads_dev // slots_dev
    query_view = queries.reshape(requests, NEW, slots_dev, grouped, HEAD_SIZE)
    scores = (
        jnp.einsum(
            "rnsgd,rksd->rnsgk",
            query_view,
            fresh_kv[:, :, :, 0, :],
            preferred_element_type=jnp.float32,
        )
        * scaling
    )
    causal = jnp.arange(NEW)[None, :] <= jnp.arange(NEW)[:, None]
    scores = jnp.where(causal[None, :, None, None, :], scores, neg_large)
    running_max = jnp.max(scores, axis=-1)
    weights = jnp.exp(scores - running_max[..., None])
    denominator = jnp.sum(weights, axis=-1)
    weighted = jnp.einsum(
        "rnsgk,rksd->rnsgd",
        weights.astype(jnp.bfloat16),
        fresh_kv[:, :, :, 1, :],
        preferred_element_type=jnp.float32,
    )
    key_width = min(PRE, 512)

    def key_step(block_index, state_carry):
        old_max, old_denominator, old_weighted = state_carry
        key_block = lax.dynamic_slice_in_dim(past_kv, block_index * key_width, key_width, 1)
        block_scores = (
            jnp.einsum(
                "rnsgd,rksd->rnsgk",
                query_view,
                key_block[:, :, :, 0, :],
                preferred_element_type=jnp.float32,
            )
            * scaling
        )
        position = block_index * key_width + jnp.arange(key_width)
        live_mask = position[None, :] < prefix_length[:, None]
        block_scores = jnp.where(live_mask[:, None, None, None, :], block_scores, neg_large)
        new_max = jnp.maximum(old_max, jnp.max(block_scores, axis=-1))
        shrink = jnp.exp(old_max - new_max)
        block_weights = jnp.exp(block_scores - new_max[..., None])
        new_denominator = old_denominator * shrink + jnp.sum(block_weights, axis=-1)
        new_weighted = old_weighted * shrink[..., None] + jnp.einsum(
            "rnsgk,rksd->rnsgd",
            block_weights.astype(jnp.bfloat16),
            key_block[:, :, :, 1, :],
            preferred_element_type=jnp.float32,
        )
        return (new_max, new_denominator, new_weighted)

    block_count = PRE // key_width
    running_max, denominator, weighted = lax.fori_loop(
        0, block_count, key_step, (running_max, denominator, weighted)
    )
    attention_output = (
        (weighted / denominator[..., None])
        .astype(jnp.bfloat16)
        .reshape(tokens, heads_dev * HEAD_SIZE)
    )
    partial_value = jnp.dot(
        attention_output,
        lax.all_gather(output_weight, ("dp", "pipe"), axis=1, tiled=True),
        preferred_element_type=jnp.float32,
    )
    projected_output = lax.psum_scatter(
        partial_value.astype(jnp.bfloat16), "tensor", scatter_dimension=1, tiled=True
    ).astype(jnp.float32)
    adapter_rows = jnp.repeat(adapter, NEW)
    selector = (adapter_rows[:, None] == jnp.arange(ADAPTER_COUNT)[None, :]).astype(jnp.float32)
    flattened_rank = jnp.dot(
        attention_output,
        adapter_down_weight.reshape(adapter_down_weight.shape[0], ADAPTER_COUNT * ADAPTER_RANK),
        preferred_element_type=jnp.float32,
    ).reshape(tokens, ADAPTER_COUNT, ADAPTER_RANK)
    partial_rank = jnp.sum(flattened_rank * selector[:, :, None], axis=1)
    pieces = lax.all_gather(partial_rank.astype(jnp.bfloat16), "tensor", axis=1, tiled=True).astype(
        partial_rank.dtype
    )
    rank_total = jnp.sum(pieces.reshape(tokens, -1, ADAPTER_RANK), axis=1)
    shrunk = rank_total.astype(jnp.bfloat16)
    spread_heads = (shrunk[:, None, :] * selector.astype(jnp.bfloat16)[:, :, None]).reshape(
        tokens, ADAPTER_COUNT * ADAPTER_RANK
    )
    adapter_output = jnp.dot(
        spread_heads,
        adapter_up_weight.reshape(ADAPTER_COUNT * ADAPTER_RANK, adapter_up_weight.shape[2]),
        preferred_element_type=jnp.float32,
    )
    combined_output = residual.astype(jnp.float32) + projected_output + adapter_output
    hidden = combined_output.astype(jnp.bfloat16)
    widened = hidden.astype(jnp.float32)
    squares = lax.psum(jnp.sum(widened * widened, axis=1), "tensor")
    inverse = lax.rsqrt(squares / MODEL_WIDTH + eps_norm)
    normed = (widened * inverse[:, None] * norm_scale_weight.astype(jnp.float32)[None, :]).astype(
        jnp.bfloat16
    )
    return (hidden, normed)


def attend_kernel(
    heads_tile,
    length_ref,
    meta_ref,
    q_ref,
    own_past,
    own_new,
    recv_past,
    recv_new,
    out_ref,
    keys,
    values,
):
    row_tile = 2
    past, new = own_past.shape[1], own_new.shape[0]

    @pl.when((pl.program_id(1) == 0) & (meta_ref[0] == 0))
    def _():
        keys[:past] = own_past[0]
        keys[past:] = own_new[...]
        values[:past] = recv_past[...]
        values[past:] = recv_new[...]

    @pl.when((pl.program_id(1) == 0) & (meta_ref[0] != 0))
    def _():
        values[:past] = own_past[0]
        values[past:] = own_new[...]
        keys[:past] = recv_past[...]
        keys[past:] = recv_new[...]

    factor = math.log2(math.e) / math.sqrt(HEAD_SIZE)
    length = length_ref[meta_ref[1]]
    live = lax.broadcasted_iota(jnp.int32, (1, past), 1) < length
    bias = jnp.where(live, 0.0, neg_large)
    rows = row_tile * new
    row = lax.broadcasted_iota(jnp.int32, (rows, new), 0) % new
    causal = lax.broadcasted_iota(jnp.int32, (rows, new), 1) <= row
    for first in range(0, heads_tile, row_tile):
        q = jnp.concatenate(
            [
                q_ref[:, h * HEAD_SIZE : (h + 1) * HEAD_SIZE]
                for h in range(first, first + row_tile)
            ],
            axis=0,
        )
        scores = lax.dot_general(
            q, keys[...], (((1,), (1,)), ((), ())), preferred_element_type=jnp.float32
        )
        old = scores[:, :past] + bias
        fresh = jnp.where(causal, scores[:, past:], neg_large)
        peak = jnp.maximum(
            jnp.max(old, axis=1, keepdims=True), jnp.max(fresh, axis=1, keepdims=True)
        )
        old = jnp.exp2((old - peak) * factor)
        fresh = jnp.exp2((fresh - peak) * factor)
        denominator = jnp.sum(old, axis=1, keepdims=True) + jnp.sum(fresh, axis=1, keepdims=True)
        mixed = jnp.dot(
            old.astype(jnp.bfloat16), values[:past], preferred_element_type=jnp.float32
        ) + jnp.dot(
            fresh.astype(jnp.bfloat16), values[past:], preferred_element_type=jnp.float32
        )
        mixed = (mixed / denominator).astype(jnp.bfloat16)
        for i in range(row_tile):
            h = first + i
            out_ref[:, h * HEAD_SIZE : (h + 1) * HEAD_SIZE] = mixed[i * new : (i + 1) * new]


def attend(request, lengths, parity, queries, cache, incoming, recv, recv_new):
    slots = recv.shape[1] // HEAD_SIZE
    heads = queries.shape[1] // HEAD_SIZE
    grouped = heads // slots
    heads_tile = min(4, grouped)
    tiles = grouped // heads_tile
    past = cache.shape[1]
    whole = past + NEW
    meta = jnp.stack([parity, jnp.int32(request)])
    width = heads_tile * HEAD_SIZE
    return pl.pallas_call(
        functools.partial(attend_kernel, heads_tile),
        out_shape=jax.ShapeDtypeStruct((NEW, heads * HEAD_SIZE), jnp.bfloat16),
        grid_spec=pltpu.PrefetchScalarGridSpec(
            num_scalar_prefetch=2,
            grid=(slots, tiles),
            in_specs=[
                pl.BlockSpec((NEW, width), lambda s, t, n, p: (request, s * tiles + t)),
                pl.BlockSpec(
                    (1, past, HEAD_SIZE), lambda s, t, n, p: (request, 0, slots * p[0] + s)
                ),
                pl.BlockSpec((NEW, HEAD_SIZE), lambda s, t, n, p: (request, slots * p[0] + s)),
                pl.BlockSpec((past, HEAD_SIZE), lambda s, t, n, p: (0, s)),
                pl.BlockSpec((NEW, HEAD_SIZE), lambda s, t, n, p: (request, s)),
            ],
            out_specs=pl.BlockSpec((NEW, width), lambda s, t, n, p: (0, s * tiles + t)),
            scratch_shapes=[
                pltpu.VMEM((whole, HEAD_SIZE), jnp.bfloat16),
                pltpu.VMEM((whole, HEAD_SIZE), jnp.bfloat16),
            ],
        ),
        compiler_params=pltpu.CompilerParams(vmem_limit_bytes=40 * 2**20),
        cost_estimate=pl.CostEstimate(
            flops=4 * NEW * heads * whole * HEAD_SIZE,
            bytes_accessed=4 * whole * slots * HEAD_SIZE + 4 * NEW * heads * HEAD_SIZE,
            transcendentals=NEW * heads * whole,
        ),
        name="attend",
    )(lengths, meta, queries, cache, incoming, recv, recv_new)


def from_others(block, axis):
    count = lax.axis_size(axis)
    return [
        lax.ppermute(block, axis, [(i, (i + shift) % count) for i in range(count)])
        for shift in range(1, count)
    ]


def shards_fast(
    queries,
    incoming_key_value,
    prefix_key_value_cache,
    prefix_length,
    adapter,
    output_weight,
    adapter_down_weight,
    adapter_up_weight,
    residual,
    norm_scale_weight,
):
    requests = prefix_length.shape[0]
    half = incoming_key_value.shape[1] // 2
    past = prefix_key_value_cache.shape[1]
    width = output_weight.shape[1]
    place = lax.axis_index("tensor")
    parity = place % 2
    upper = place // 2
    x = lax.axis_index("dp")
    core = lax.axis_index("pipe")
    send_at = (1 - parity) * half
    outgoing = [
        lax.dynamic_slice(prefix_key_value_cache, (r, 0, send_at), (1, past, half))[0]
        for r in range(requests)
    ]
    outgoing_new = lax.dynamic_slice(
        incoming_key_value, (0, send_at), (incoming_key_value.shape[0], half)
    )
    arrived_new = partner(outgoing_new, "tensor", 0)
    arrived = [partner(block, "tensor", 0) for block in outgoing]
    weight_partner = partner(output_weight, "pipe", 0)
    down = adapter_down_weight.reshape(adapter_down_weight.shape[0], ADAPTER_COUNT * ADAPTER_RANK)

    keep_own = parity == core
    weight_keep = jnp.where(keep_own, output_weight, weight_partner)
    weight_send = jnp.where(keep_own, weight_partner, output_weight)
    weight_keep, weight_send, arrived[0] = lax.optimization_barrier(
        (weight_keep, weight_send, arrived[0])
    )

    def product(rows, weight):
        return jnp.dot(rows, weight, preferred_element_type=jnp.float32).astype(jnp.bfloat16)

    state = []
    for r in range(requests):
        attended = attend(
            r,
            prefix_length,
            parity,
            queries,
            prefix_key_value_cache,
            incoming_key_value,
            arrived[r],
            arrived_new,
        )
        across = partner(attended, "dp", 0)
        flat = jnp.dot(attended, down, preferred_element_type=jnp.float32)
        rank = lax.dynamic_slice(
            flat, (0, adapter[r] * ADAPTER_RANK), (NEW, ADAPTER_RANK)
        ).astype(jnp.bfloat16)
        rank = jnp.pad(rank, ((0, 0), (0, HEAD_SIZE - ADAPTER_RANK)))
        payload = jnp.concatenate([product(attended, weight_send), rank], axis=1)
        got_mine = partner(payload, "tensor", 0)
        keep_mine = product(attended, weight_keep)
        sent_theirs = product(across, weight_send)
        if r + 1 < requests:
            keep_mine, arrived[r + 1], _ = lax.optimization_barrier(
                (keep_mine, arrived[r + 1], sent_theirs)
            )
        got_theirs = partner(sent_theirs, "tensor", 0)
        keep_theirs = product(across, weight_keep)
        keep_mine, keep_theirs = lax.optimization_barrier((keep_mine, keep_theirs))
        state.append((rank, keep_mine, keep_theirs, got_mine, got_theirs))

    hidden = []
    for r in range(requests):
        rank, keep_mine, keep_theirs, got_mine, got_theirs = state[r]
        if r > 0:
            got_mine, got_theirs, _ = lax.optimization_barrier((got_mine, got_theirs, got_first))
        theirs_pair = (keep_theirs.astype(jnp.float32) + got_theirs.astype(jnp.float32)).astype(
            jnp.bfloat16
        )
        theirs = partner(theirs_pair, "dp", 0)
        mine = (keep_mine.astype(jnp.float32) + got_mine[:, :width].astype(jnp.float32)).astype(
            jnp.bfloat16
        )
        rank_pair = (rank.astype(jnp.float32) + got_mine[:, width:].astype(jnp.float32)).astype(
            jnp.bfloat16
        )
        last_kept = jnp.where(x == upper, mine, theirs)
        last_sent = jnp.concatenate([jnp.where(x == upper, theirs, mine), rank_pair], axis=1)
        if r + 1 < requests:
            got_first = partner(last_sent[:, : width // 2], "tensor", 1)
            got_rest = partner(last_sent[:, width // 2 :], "tensor", 1)
            last_got = jnp.concatenate([got_first, got_rest], axis=1)
        else:
            last_got = partner(last_sent, "tensor", 1)
        projected = last_kept.astype(jnp.float32) + last_got[:, :width].astype(jnp.float32)
        shrunk = (rank_pair.astype(jnp.float32) + last_got[:, width:].astype(jnp.float32)).astype(
            jnp.bfloat16
        )
        up = lax.dynamic_slice(
            adapter_up_weight, (adapter[r], 0, 0), (1, ADAPTER_RANK, width)
        )[0]
        adapter_output = jnp.dot(shrunk[:, :ADAPTER_RANK], up, preferred_element_type=jnp.float32)
        rows = residual[r * NEW : (r + 1) * NEW].astype(jnp.float32)
        hidden.append((rows + projected + adapter_output).astype(jnp.bfloat16))
    hidden = jnp.concatenate(hidden, axis=0)
    widened = hidden.astype(jnp.float32)
    own_squares = jnp.sum(widened * widened, axis=1)
    squares = own_squares
    for piece in from_others(own_squares, "tensor"):
        squares = squares + piece
    inverse = lax.rsqrt(squares / MODEL_WIDTH + eps_norm)
    normed = (widened * inverse[:, None] * norm_scale_weight.astype(jnp.float32)[None, :]).astype(
        jnp.bfloat16
    )
    return (hidden, normed)


def solution(mesh):
    sizes = tuple(mesh.shape[name] for name in ("tensor", "dp", "pipe"))
    shards = shards_fast if sizes == (4, 2, 2) else shards_any
    return jax.shard_map(
        shards,
        mesh=mesh,
        in_specs=(
            P(("groups", "dp", "pipe"), "tensor"),
            P(("groups", "dp", "pipe"), "tensor"),
            P(("groups", "dp", "pipe"), None, "tensor"),
            P(("groups", "dp", "pipe")),
            P(("groups", "dp", "pipe")),
            P("tensor", ("dp", "pipe")),
            P("tensor", None, None),
            P(None, None, "tensor"),
            P(("groups", "dp", "pipe"), "tensor"),
            P("tensor"),
        ),
        out_specs=(P(("groups", "dp", "pipe"), "tensor"), P(("groups", "dp", "pipe"), "tensor")),
        check_vma=False,
    )
```

```python
import functools
import math

import jax
import jax.numpy as jnp
from jax import lax
from jax.experimental import pallas as pl
from jax.experimental.pallas import tpu as pltpu
from jax.sharding import PartitionSpec as P

MODEL_WIDTH = 8192
HEAD_SIZE = 128
ADAPTER_RANK = 64
ADAPTER_COUNT = 4
NEW = 128
PRE = 2048


neg_large = -1e30
eps_norm = 1e-05


def partner(block, axis, distance):
    count = lax.axis_size(axis)
    route = []
    for low in range(count):
        high = low | 1 << distance
        if high != low and high < count:
            route += [(low, high), (high, low)]
    return lax.ppermute(block, axis, route)


def shards_any(
    queries,
    incoming_key_value,
    prefix_key_value_cache,
    prefix_length,
    adapter,
    output_weight,
    adapter_down_weight,
    adapter_up_weight,
    residual,
    norm_scale_weight,
):
    requests = prefix_length.shape[0]
    tokens = queries.shape[0]
    heads_dev = queries.shape[1] // HEAD_SIZE
    block_heads = incoming_key_value.shape[1] // HEAD_SIZE
    scaling = 1.0 / math.sqrt(HEAD_SIZE)
    partner_new, partner_past = partner((incoming_key_value, prefix_key_value_cache), "tensor", 0)
    parity = lax.axis_index("tensor") % 2
    holds_keys = parity == 0
    fresh_keys = jnp.where(holds_keys, incoming_key_value, partner_new).reshape(
        requests, NEW, block_heads, HEAD_SIZE
    )
    fresh_values = jnp.where(holds_keys, partner_new, incoming_key_value).reshape(
        requests, NEW, block_heads, HEAD_SIZE
    )
    past_keys = jnp.where(holds_keys, prefix_key_value_cache, partner_past).reshape(
        requests, PRE, block_heads, HEAD_SIZE
    )
    past_values = jnp.where(holds_keys, partner_past, prefix_key_value_cache).reshape(
        requests, PRE, block_heads, HEAD_SIZE
    )
    slots_dev = max(1, block_heads // 2)
    offset = parity * (block_heads - slots_dev)
    fresh_kv = jnp.stack(
        [
            lax.dynamic_slice_in_dim(fresh_keys, offset, slots_dev, 2),
            lax.dynamic_slice_in_dim(fresh_values, offset, slots_dev, 2),
        ],
        axis=3,
    )
    past_kv = jnp.stack(
        [
            lax.dynamic_slice_in_dim(past_keys, offset, slots_dev, 2),
            lax.dynamic_slice_in_dim(past_values, offset, slots_dev, 2),
        ],
        axis=3,
    )
    grouped = heads_dev // slots_dev
    query_view = queries.reshape(requests, NEW, slots_dev, grouped, HEAD_SIZE)
    scores = (
        jnp.einsum(
            "rnsgd,rksd->rnsgk",
            query_view,
            fresh_kv[:, :, :, 0, :],
            preferred_element_type=jnp.float32,
        )
        * scaling
    )
    causal = jnp.arange(NEW)[None, :] <= jnp.arange(NEW)[:, None]
    scores = jnp.where(causal[None, :, None, None, :], scores, neg_large)
    running_max = jnp.max(scores, axis=-1)
    weights = jnp.exp(scores - running_max[..., None])
    denominator = jnp.sum(weights, axis=-1)
    weighted = jnp.einsum(
        "rnsgk,rksd->rnsgd",
        weights.astype(jnp.bfloat16),
        fresh_kv[:, :, :, 1, :],
        preferred_element_type=jnp.float32,
    )
    key_width = min(PRE, 512)

    def key_step(block_index, state_carry):
        old_max, old_denominator, old_weighted = state_carry
        key_block = lax.dynamic_slice_in_dim(past_kv, block_index * key_width, key_width, 1)
        block_scores = (
            jnp.einsum(
                "rnsgd,rksd->rnsgk",
                query_view,
                key_block[:, :, :, 0, :],
                preferred_element_type=jnp.float32,
            )
            * scaling
        )
        position = block_index * key_width + jnp.arange(key_width)
        live_mask = position[None, :] < prefix_length[:, None]
        block_scores = jnp.where(live_mask[:, None, None, None, :], block_scores, neg_large)
        new_max = jnp.maximum(old_max, jnp.max(block_scores, axis=-1))
        shrink = jnp.exp(old_max - new_max)
        block_weights = jnp.exp(block_scores - new_max[..., None])
        new_denominator = old_denominator * shrink + jnp.sum(block_weights, axis=-1)
        new_weighted = old_weighted * shrink[..., None] + jnp.einsum(
            "rnsgk,rksd->rnsgd",
            block_weights.astype(jnp.bfloat16),
            key_block[:, :, :, 1, :],
            preferred_element_type=jnp.float32,
        )
        return (new_max, new_denominator, new_weighted)

    block_count = PRE // key_width
    running_max, denominator, weighted = lax.fori_loop(
        0, block_count, key_step, (running_max, denominator, weighted)
    )
    attention_output = (
        (weighted / denominator[..., None])
        .astype(jnp.bfloat16)
        .reshape(tokens, heads_dev * HEAD_SIZE)
    )
    partial_value = jnp.dot(
        attention_output,
        lax.all_gather(output_weight, ("dp", "pipe"), axis=1, tiled=True),
        preferred_element_type=jnp.float32,
    )
    projected_output = lax.psum_scatter(
        partial_value.astype(jnp.bfloat16), "tensor", scatter_dimension=1, tiled=True
    ).astype(jnp.float32)
    adapter_rows = jnp.repeat(adapter, NEW)
    selector = (adapter_rows[:, None] == jnp.arange(ADAPTER_COUNT)[None, :]).astype(jnp.float32)
    flattened_rank = jnp.dot(
        attention_output,
        adapter_down_weight.reshape(adapter_down_weight.shape[0], ADAPTER_COUNT * ADAPTER_RANK),
        preferred_element_type=jnp.float32,
    ).reshape(tokens, ADAPTER_COUNT, ADAPTER_RANK)
    partial_rank = jnp.sum(flattened_rank * selector[:, :, None], axis=1)
    pieces = lax.all_gather(partial_rank.astype(jnp.bfloat16), "tensor", axis=1, tiled=True).astype(
        partial_rank.dtype
    )
    rank_total = jnp.sum(pieces.reshape(tokens, -1, ADAPTER_RANK), axis=1)
    shrunk = rank_total.astype(jnp.bfloat16)
    spread_heads = (shrunk[:, None, :] * selector.astype(jnp.bfloat16)[:, :, None]).reshape(
        tokens, ADAPTER_COUNT * ADAPTER_RANK
    )
    adapter_output = jnp.dot(
        spread_heads,
        adapter_up_weight.reshape(ADAPTER_COUNT * ADAPTER_RANK, adapter_up_weight.shape[2]),
        preferred_element_type=jnp.float32,
    )
    combined_output = residual.astype(jnp.float32) + projected_output + adapter_output
    hidden = combined_output.astype(jnp.bfloat16)
    widened = hidden.astype(jnp.float32)
    squares = lax.psum(jnp.sum(widened * widened, axis=1), "tensor")
    inverse = lax.rsqrt(squares / MODEL_WIDTH + eps_norm)
    normed = (widened * inverse[:, None] * norm_scale_weight.astype(jnp.float32)[None, :]).astype(
        jnp.bfloat16
    )
    return (hidden, normed)


def attend_kernel(
    heads_tile,
    length_ref,
    meta_ref,
    q_ref,
    own_past,
    own_new,
    recv_past,
    recv_new,
    out_ref,
    keys,
    values,
):
    row_tile = 2
    past, new = own_past.shape[1], own_new.shape[0]

    @pl.when((pl.program_id(1) == 0) & (meta_ref[0] == 0))
    def _():
        keys[:past] = own_past[0]
        keys[past:] = own_new[...]
        values[:past] = recv_past[...]
        values[past:] = recv_new[...]

    @pl.when((pl.program_id(1) == 0) & (meta_ref[0] != 0))
    def _():
        values[:past] = own_past[0]
        values[past:] = own_new[...]
        keys[:past] = recv_past[...]
        keys[past:] = recv_new[...]

    factor = math.log2(math.e) / math.sqrt(HEAD_SIZE)
    length = length_ref[meta_ref[1]]
    live = lax.broadcasted_iota(jnp.int32, (1, past), 1) < length
    bias = jnp.where(live, 0.0, neg_large)
    rows = row_tile * new
    row = lax.broadcasted_iota(jnp.int32, (rows, new), 0) % new
    causal = lax.broadcasted_iota(jnp.int32, (rows, new), 1) <= row
    for first in range(0, heads_tile, row_tile):
        q = jnp.concatenate(
            [
                q_ref[:, h * HEAD_SIZE : (h + 1) * HEAD_SIZE]
                for h in range(first, first + row_tile)
            ],
            axis=0,
        )
        scores = lax.dot_general(
            q, keys[...], (((1,), (1,)), ((), ())), preferred_element_type=jnp.float32
        )
        old = scores[:, :past] + bias
        fresh = jnp.where(causal, scores[:, past:], neg_large)
        peak = jnp.maximum(
            jnp.max(old, axis=1, keepdims=True), jnp.max(fresh, axis=1, keepdims=True)
        )
        old = jnp.exp2((old - peak) * factor)
        fresh = jnp.exp2((fresh - peak) * factor)
        denominator = jnp.sum(old, axis=1, keepdims=True) + jnp.sum(fresh, axis=1, keepdims=True)
        mixed = jnp.dot(
            old.astype(jnp.bfloat16), values[:past], preferred_element_type=jnp.float32
        ) + jnp.dot(
            fresh.astype(jnp.bfloat16), values[past:], preferred_element_type=jnp.float32
        )
        mixed = (mixed / denominator).astype(jnp.bfloat16)
        for i in range(row_tile):
            h = first + i
            out_ref[:, h * HEAD_SIZE : (h + 1) * HEAD_SIZE] = mixed[i * new : (i + 1) * new]


def attend(request, lengths, parity, queries, cache, incoming, recv, recv_new):
    slots = recv.shape[1] // HEAD_SIZE
    heads = queries.shape[1] // HEAD_SIZE
    grouped = heads // slots
    heads_tile = min(4, grouped)
    tiles = grouped // heads_tile
    past = cache.shape[1]
    whole = past + NEW
    meta = jnp.stack([parity, jnp.int32(request)])
    width = heads_tile * HEAD_SIZE
    return pl.pallas_call(
        functools.partial(attend_kernel, heads_tile),
        out_shape=jax.ShapeDtypeStruct((NEW, heads * HEAD_SIZE), jnp.bfloat16),
        grid_spec=pltpu.PrefetchScalarGridSpec(
            num_scalar_prefetch=2,
            grid=(slots, tiles),
            in_specs=[
                pl.BlockSpec((NEW, width), lambda s, t, n, p: (request, s * tiles + t)),
                pl.BlockSpec(
                    (1, past, HEAD_SIZE), lambda s, t, n, p: (request, 0, slots * p[0] + s)
                ),
                pl.BlockSpec((NEW, HEAD_SIZE), lambda s, t, n, p: (request, slots * p[0] + s)),
                pl.BlockSpec((past, HEAD_SIZE), lambda s, t, n, p: (0, s)),
                pl.BlockSpec((NEW, HEAD_SIZE), lambda s, t, n, p: (request, s)),
            ],
            out_specs=pl.BlockSpec((NEW, width), lambda s, t, n, p: (0, s * tiles + t)),
            scratch_shapes=[
                pltpu.VMEM((whole, HEAD_SIZE), jnp.bfloat16),
                pltpu.VMEM((whole, HEAD_SIZE), jnp.bfloat16),
            ],
        ),
        compiler_params=pltpu.CompilerParams(vmem_limit_bytes=40 * 2**20),
        cost_estimate=pl.CostEstimate(
            flops=4 * NEW * heads * whole * HEAD_SIZE,
            bytes_accessed=4 * whole * slots * HEAD_SIZE + 4 * NEW * heads * HEAD_SIZE,
            transcendentals=NEW * heads * whole,
        ),
        name="attend",
    )(lengths, meta, queries, cache, incoming, recv, recv_new)


def from_others(block, axis):
    count = lax.axis_size(axis)
    return [
        lax.ppermute(block, axis, [(i, (i + shift) % count) for i in range(count)])
        for shift in range(1, count)
    ]


def shards_fast(
    queries,
    incoming_key_value,
    prefix_key_value_cache,
    prefix_length,
    adapter,
    output_weight,
    adapter_down_weight,
    adapter_up_weight,
    residual,
    norm_scale_weight,
):
    requests = prefix_length.shape[0]
    half = incoming_key_value.shape[1] // 2
    past = prefix_key_value_cache.shape[1]
    width = output_weight.shape[1]
    place = lax.axis_index("tensor")
    parity = place % 2
    upper = place // 2
    x = lax.axis_index("dp")
    core = lax.axis_index("pipe")
    send_at = (1 - parity) * half
    outgoing = [
        lax.dynamic_slice(prefix_key_value_cache, (r, 0, send_at), (1, past, half))[0]
        for r in range(requests)
    ]
    outgoing_new = lax.dynamic_slice(
        incoming_key_value, (0, send_at), (incoming_key_value.shape[0], half)
    )
    arrived_new = partner(outgoing_new, "tensor", 0)
    arrived = [partner(block, "tensor", 0) for block in outgoing]
    weight_partner = partner(output_weight, "pipe", 0)
    down = adapter_down_weight.reshape(adapter_down_weight.shape[0], ADAPTER_COUNT * ADAPTER_RANK)

    keep_own = parity == core
    weight_keep = jnp.where(keep_own, output_weight, weight_partner)
    weight_send = jnp.where(keep_own, weight_partner, output_weight)
    weight_keep, weight_send, arrived[0] = lax.optimization_barrier(
        (weight_keep, weight_send, arrived[0])
    )

    def product(rows, weight):
        return jnp.dot(rows, weight, preferred_element_type=jnp.float32).astype(jnp.bfloat16)

    cuts = [slice(0, width // 2), slice(width // 2, width)]
    state = []
    for r in range(requests):
        attended = attend(
            r,
            prefix_length,
            parity,
            queries,
            prefix_key_value_cache,
            incoming_key_value,
            arrived[r],
            arrived_new,
        )
        across = partner(attended, "dp", 0)
        flat = jnp.dot(attended, down, preferred_element_type=jnp.float32)
        rank = lax.dynamic_slice(
            flat, (0, adapter[r] * ADAPTER_RANK), (NEW, ADAPTER_RANK)
        ).astype(jnp.bfloat16)
        rank = jnp.pad(rank, ((0, 0), (0, HEAD_SIZE - ADAPTER_RANK)))
        payload = jnp.concatenate([product(attended, weight_send), rank], axis=1)
        got_mine = partner(payload, "tensor", 0)
        keep_mine = product(attended, weight_keep)
        sent_theirs = product(across, weight_send)
        sent_theirs = [sent_theirs[:, cut] for cut in cuts]
        if r + 1 < requests:
            keep_mine, arrived[r + 1], _ = lax.optimization_barrier(
                (keep_mine, arrived[r + 1], sent_theirs)
            )
        got_theirs = [partner(block, "tensor", 0) for block in sent_theirs]
        keep_theirs = product(across, weight_keep)
        keep_mine, keep_theirs = lax.optimization_barrier((keep_mine, keep_theirs))
        state.append((rank, keep_mine, keep_theirs, got_mine, got_theirs))

    def pair_sum(kept, got):
        return (kept.astype(jnp.float32) + got.astype(jnp.float32)).astype(jnp.bfloat16)

    hidden = []
    before = None
    for r in range(requests):
        rank, keep_mine, keep_theirs, got_mine, got_theirs = state[r]
        if before is not None:
            got_mine, got_theirs[0], _ = lax.optimization_barrier(
                (got_mine, got_theirs[0], (before[0], payload))
            )
            got_theirs[1], _ = lax.optimization_barrier((got_theirs[1], before[1]))
        rank_pair = pair_sum(rank, got_mine[:, width:])
        kept, before = [], []
        for i, cut in enumerate(cuts):
            if i > 0:
                got_theirs[i], _ = lax.optimization_barrier((got_theirs[i], crossing))
            crossing = pair_sum(keep_theirs[:, cut], got_theirs[i])
            theirs = partner(crossing, "dp", 0)
            if i > 0:
                theirs, _ = lax.optimization_barrier((theirs, payload))
            mine = pair_sum(keep_mine[:, cut], got_mine[:, cut])
            kept.append(jnp.where(x == upper, mine, theirs))
            payload = jnp.where(x == upper, theirs, mine)
            if i == 0:
                payload = jnp.concatenate([payload, rank_pair], axis=1)
            before.append(partner(payload, "tensor", 1))
        shrunk = pair_sum(rank_pair, before[0][:, width // 2 :])[:, :ADAPTER_RANK]
        up = lax.dynamic_slice(
            adapter_up_weight, (adapter[r], 0, 0), (1, ADAPTER_RANK, width)
        )[0]
        pieces = []
        for i, cut in enumerate(cuts):
            got = before[i][:, : width // 2].astype(jnp.float32)
            projected = kept[i].astype(jnp.float32) + got
            adapter_output = jnp.dot(shrunk, up[:, cut], preferred_element_type=jnp.float32)
            rows = residual[r * NEW : (r + 1) * NEW, cut].astype(jnp.float32)
            pieces.append((rows + projected + adapter_output).astype(jnp.bfloat16))
        hidden.append(jnp.concatenate(pieces, axis=1))
    hidden = jnp.concatenate(hidden, axis=0)
    widened = hidden.astype(jnp.float32)
    own_squares = jnp.sum(widened * widened, axis=1)
    squares = own_squares
    for piece in from_others(own_squares, "tensor"):
        squares = squares + piece
    inverse = lax.rsqrt(squares / MODEL_WIDTH + eps_norm)
    normed = (widened * inverse[:, None] * norm_scale_weight.astype(jnp.float32)[None, :]).astype(
        jnp.bfloat16
    )
    return (hidden, normed)


def solution(mesh):
    sizes = tuple(mesh.shape[name] for name in ("tensor", "dp", "pipe"))
    shards = shards_fast if sizes == (4, 2, 2) else shards_any
    return jax.shard_map(
        shards,
        mesh=mesh,
        in_specs=(
            P(("groups", "dp", "pipe"), "tensor"),
            P(("groups", "dp", "pipe"), "tensor"),
            P(("groups", "dp", "pipe"), None, "tensor"),
            P(("groups", "dp", "pipe")),
            P(("groups", "dp", "pipe")),
            P("tensor", ("dp", "pipe")),
            P("tensor", None, None),
            P(None, None, "tensor"),
            P(("groups", "dp", "pipe"), "tensor"),
            P("tensor"),
        ),
        out_specs=(P(("groups", "dp", "pipe"), "tensor"), P(("groups", "dp", "pipe"), "tensor")),
        check_vma=False,
    )
```

```python
import functools
import math

import jax
import jax.numpy as jnp
from jax import lax
from jax.experimental import pallas as pl
from jax.experimental.pallas import tpu as pltpu
from jax.sharding import PartitionSpec as P

MODEL_WIDTH = 8192
HEAD_SIZE = 128
ADAPTER_RANK = 64
ADAPTER_COUNT = 4
NEW = 128
PRE = 2048


neg_large = -1e30
eps_norm = 1e-05


def partner(block, axis, distance):
    count = lax.axis_size(axis)
    route = []
    for low in range(count):
        high = low | 1 << distance
        if high != low and high < count:
            route += [(low, high), (high, low)]
    return lax.ppermute(block, axis, route)


def shards_any(
    queries,
    incoming_key_value,
    prefix_key_value_cache,
    prefix_length,
    adapter,
    output_weight,
    adapter_down_weight,
    adapter_up_weight,
    residual,
    norm_scale_weight,
):
    requests = prefix_length.shape[0]
    tokens = queries.shape[0]
    heads_dev = queries.shape[1] // HEAD_SIZE
    block_heads = incoming_key_value.shape[1] // HEAD_SIZE
    scaling = 1.0 / math.sqrt(HEAD_SIZE)
    partner_new, partner_past = partner((incoming_key_value, prefix_key_value_cache), "tensor", 0)
    parity = lax.axis_index("tensor") % 2
    holds_keys = parity == 0
    fresh_keys = jnp.where(holds_keys, incoming_key_value, partner_new).reshape(
        requests, NEW, block_heads, HEAD_SIZE
    )
    fresh_values = jnp.where(holds_keys, partner_new, incoming_key_value).reshape(
        requests, NEW, block_heads, HEAD_SIZE
    )
    past_keys = jnp.where(holds_keys, prefix_key_value_cache, partner_past).reshape(
        requests, PRE, block_heads, HEAD_SIZE
    )
    past_values = jnp.where(holds_keys, partner_past, prefix_key_value_cache).reshape(
        requests, PRE, block_heads, HEAD_SIZE
    )
    slots_dev = max(1, block_heads // 2)
    offset = parity * (block_heads - slots_dev)
    fresh_kv = jnp.stack(
        [
            lax.dynamic_slice_in_dim(fresh_keys, offset, slots_dev, 2),
            lax.dynamic_slice_in_dim(fresh_values, offset, slots_dev, 2),
        ],
        axis=3,
    )
    past_kv = jnp.stack(
        [
            lax.dynamic_slice_in_dim(past_keys, offset, slots_dev, 2),
            lax.dynamic_slice_in_dim(past_values, offset, slots_dev, 2),
        ],
        axis=3,
    )
    grouped = heads_dev // slots_dev
    query_view = queries.reshape(requests, NEW, slots_dev, grouped, HEAD_SIZE)
    scores = (
        jnp.einsum(
            "rnsgd,rksd->rnsgk",
            query_view,
            fresh_kv[:, :, :, 0, :],
            preferred_element_type=jnp.float32,
        )
        * scaling
    )
    causal = jnp.arange(NEW)[None, :] <= jnp.arange(NEW)[:, None]
    scores = jnp.where(causal[None, :, None, None, :], scores, neg_large)
    running_max = jnp.max(scores, axis=-1)
    weights = jnp.exp(scores - running_max[..., None])
    denominator = jnp.sum(weights, axis=-1)
    weighted = jnp.einsum(
        "rnsgk,rksd->rnsgd",
        weights.astype(jnp.bfloat16),
        fresh_kv[:, :, :, 1, :],
        preferred_element_type=jnp.float32,
    )
    key_width = min(PRE, 512)

    def key_step(block_index, state_carry):
        old_max, old_denominator, old_weighted = state_carry
        key_block = lax.dynamic_slice_in_dim(past_kv, block_index * key_width, key_width, 1)
        block_scores = (
            jnp.einsum(
                "rnsgd,rksd->rnsgk",
                query_view,
                key_block[:, :, :, 0, :],
                preferred_element_type=jnp.float32,
            )
            * scaling
        )
        position = block_index * key_width + jnp.arange(key_width)
        live_mask = position[None, :] < prefix_length[:, None]
        block_scores = jnp.where(live_mask[:, None, None, None, :], block_scores, neg_large)
        new_max = jnp.maximum(old_max, jnp.max(block_scores, axis=-1))
        shrink = jnp.exp(old_max - new_max)
        block_weights = jnp.exp(block_scores - new_max[..., None])
        new_denominator = old_denominator * shrink + jnp.sum(block_weights, axis=-1)
        new_weighted = old_weighted * shrink[..., None] + jnp.einsum(
            "rnsgk,rksd->rnsgd",
            block_weights.astype(jnp.bfloat16),
            key_block[:, :, :, 1, :],
            preferred_element_type=jnp.float32,
        )
        return (new_max, new_denominator, new_weighted)

    block_count = PRE // key_width
    running_max, denominator, weighted = lax.fori_loop(
        0, block_count, key_step, (running_max, denominator, weighted)
    )
    attention_output = (
        (weighted / denominator[..., None])
        .astype(jnp.bfloat16)
        .reshape(tokens, heads_dev * HEAD_SIZE)
    )
    partial_value = jnp.dot(
        attention_output,
        lax.all_gather(output_weight, ("dp", "pipe"), axis=1, tiled=True),
        preferred_element_type=jnp.float32,
    )
    projected_output = lax.psum_scatter(
        partial_value.astype(jnp.bfloat16), "tensor", scatter_dimension=1, tiled=True
    ).astype(jnp.float32)
    adapter_rows = jnp.repeat(adapter, NEW)
    selector = (adapter_rows[:, None] == jnp.arange(ADAPTER_COUNT)[None, :]).astype(jnp.float32)
    flattened_rank = jnp.dot(
        attention_output,
        adapter_down_weight.reshape(adapter_down_weight.shape[0], ADAPTER_COUNT * ADAPTER_RANK),
        preferred_element_type=jnp.float32,
    ).reshape(tokens, ADAPTER_COUNT, ADAPTER_RANK)
    partial_rank = jnp.sum(flattened_rank * selector[:, :, None], axis=1)
    pieces = lax.all_gather(partial_rank.astype(jnp.bfloat16), "tensor", axis=1, tiled=True).astype(
        partial_rank.dtype
    )
    rank_total = jnp.sum(pieces.reshape(tokens, -1, ADAPTER_RANK), axis=1)
    shrunk = rank_total.astype(jnp.bfloat16)
    spread_heads = (shrunk[:, None, :] * selector.astype(jnp.bfloat16)[:, :, None]).reshape(
        tokens, ADAPTER_COUNT * ADAPTER_RANK
    )
    adapter_output = jnp.dot(
        spread_heads,
        adapter_up_weight.reshape(ADAPTER_COUNT * ADAPTER_RANK, adapter_up_weight.shape[2]),
        preferred_element_type=jnp.float32,
    )
    combined_output = residual.astype(jnp.float32) + projected_output + adapter_output
    hidden = combined_output.astype(jnp.bfloat16)
    widened = hidden.astype(jnp.float32)
    squares = lax.psum(jnp.sum(widened * widened, axis=1), "tensor")
    inverse = lax.rsqrt(squares / MODEL_WIDTH + eps_norm)
    normed = (widened * inverse[:, None] * norm_scale_weight.astype(jnp.float32)[None, :]).astype(
        jnp.bfloat16
    )
    return (hidden, normed)


def attend_kernel(
    heads_tile,
    length_ref,
    meta_ref,
    q_ref,
    own_past,
    own_new,
    recv_past,
    recv_new,
    out_ref,
    keys,
    values,
):
    row_tile = 2
    past, new = own_past.shape[1], own_new.shape[0]

    @pl.when((pl.program_id(1) == 0) & (meta_ref[0] == 0))
    def _():
        keys[:past] = own_past[0]
        keys[past:] = own_new[...]
        values[:past] = recv_past[...]
        values[past:] = recv_new[...]

    @pl.when((pl.program_id(1) == 0) & (meta_ref[0] != 0))
    def _():
        values[:past] = own_past[0]
        values[past:] = own_new[...]
        keys[:past] = recv_past[...]
        keys[past:] = recv_new[...]

    factor = math.log2(math.e) / math.sqrt(HEAD_SIZE)
    length = length_ref[meta_ref[1]]
    live = lax.broadcasted_iota(jnp.int32, (1, past), 1) < length
    bias = jnp.where(live, 0.0, neg_large)
    rows = row_tile * new
    row = lax.broadcasted_iota(jnp.int32, (rows, new), 0) % new
    causal = lax.broadcasted_iota(jnp.int32, (rows, new), 1) <= row
    for first in range(0, heads_tile, row_tile):
        q = jnp.concatenate(
            [
                q_ref[:, h * HEAD_SIZE : (h + 1) * HEAD_SIZE]
                for h in range(first, first + row_tile)
            ],
            axis=0,
        )
        scores = lax.dot_general(
            q, keys[...], (((1,), (1,)), ((), ())), preferred_element_type=jnp.float32
        )
        old = scores[:, :past] + bias
        fresh = jnp.where(causal, scores[:, past:], neg_large)
        peak = jnp.maximum(
            jnp.max(old, axis=1, keepdims=True), jnp.max(fresh, axis=1, keepdims=True)
        )
        old = jnp.exp2((old - peak) * factor)
        fresh = jnp.exp2((fresh - peak) * factor)
        denominator = jnp.sum(old, axis=1, keepdims=True) + jnp.sum(fresh, axis=1, keepdims=True)
        mixed = jnp.dot(
            old.astype(jnp.bfloat16), values[:past], preferred_element_type=jnp.float32
        ) + jnp.dot(
            fresh.astype(jnp.bfloat16), values[past:], preferred_element_type=jnp.float32
        )
        mixed = (mixed / denominator).astype(jnp.bfloat16)
        for i in range(row_tile):
            h = first + i
            out_ref[:, h * HEAD_SIZE : (h + 1) * HEAD_SIZE] = mixed[i * new : (i + 1) * new]


def attend(request, lengths, parity, queries, cache, incoming, recv, recv_new):
    slots = recv.shape[1] // HEAD_SIZE
    heads = queries.shape[1] // HEAD_SIZE
    grouped = heads // slots
    heads_tile = min(4, grouped)
    tiles = grouped // heads_tile
    past = cache.shape[1]
    whole = past + NEW
    meta = jnp.stack([parity, jnp.int32(request)])
    width = heads_tile * HEAD_SIZE
    return pl.pallas_call(
        functools.partial(attend_kernel, heads_tile),
        out_shape=jax.ShapeDtypeStruct((NEW, heads * HEAD_SIZE), jnp.bfloat16),
        grid_spec=pltpu.PrefetchScalarGridSpec(
            num_scalar_prefetch=2,
            grid=(slots, tiles),
            in_specs=[
                pl.BlockSpec((NEW, width), lambda s, t, n, p: (request, s * tiles + t)),
                pl.BlockSpec(
                    (1, past, HEAD_SIZE), lambda s, t, n, p: (request, 0, slots * p[0] + s)
                ),
                pl.BlockSpec((NEW, HEAD_SIZE), lambda s, t, n, p: (request, slots * p[0] + s)),
                pl.BlockSpec((past, HEAD_SIZE), lambda s, t, n, p: (0, s)),
                pl.BlockSpec((NEW, HEAD_SIZE), lambda s, t, n, p: (request, s)),
            ],
            out_specs=pl.BlockSpec((NEW, width), lambda s, t, n, p: (0, s * tiles + t)),
            scratch_shapes=[
                pltpu.VMEM((whole, HEAD_SIZE), jnp.bfloat16),
                pltpu.VMEM((whole, HEAD_SIZE), jnp.bfloat16),
            ],
        ),
        compiler_params=pltpu.CompilerParams(vmem_limit_bytes=40 * 2**20),
        cost_estimate=pl.CostEstimate(
            flops=4 * NEW * heads * whole * HEAD_SIZE,
            bytes_accessed=4 * whole * slots * HEAD_SIZE + 4 * NEW * heads * HEAD_SIZE,
            transcendentals=NEW * heads * whole,
        ),
        name="attend",
    )(lengths, meta, queries, cache, incoming, recv, recv_new)


def from_others(block, axis):
    count = lax.axis_size(axis)
    return [
        lax.ppermute(block, axis, [(i, (i + shift) % count) for i in range(count)])
        for shift in range(1, count)
    ]


def shards_fast(
    queries,
    incoming_key_value,
    prefix_key_value_cache,
    prefix_length,
    adapter,
    output_weight,
    adapter_down_weight,
    adapter_up_weight,
    residual,
    norm_scale_weight,
):
    requests = prefix_length.shape[0]
    half = incoming_key_value.shape[1] // 2
    past = prefix_key_value_cache.shape[1]
    width = output_weight.shape[1]
    place = lax.axis_index("tensor")
    parity = place % 2
    upper = place // 2
    x = lax.axis_index("dp")
    core = lax.axis_index("pipe")
    send_at = (1 - parity) * half
    outgoing = [
        lax.dynamic_slice(prefix_key_value_cache, (r, 0, send_at), (1, past, half))[0]
        for r in range(requests)
    ]
    outgoing_new = lax.dynamic_slice(
        incoming_key_value, (0, send_at), (incoming_key_value.shape[0], half)
    )
    arrived_new = partner(outgoing_new, "tensor", 0)
    arrived = [partner(block, "tensor", 0) for block in outgoing]
    weight_partner = partner(output_weight, "pipe", 0)
    down = adapter_down_weight.reshape(adapter_down_weight.shape[0], ADAPTER_COUNT * ADAPTER_RANK)

    keep_own = parity == core
    weight_keep = jnp.where(keep_own, output_weight, weight_partner)
    weight_send = jnp.where(keep_own, weight_partner, output_weight)
    weight_keep, weight_send, arrived[0] = lax.optimization_barrier(
        (weight_keep, weight_send, arrived[0])
    )

    def product(rows, weight):
        return jnp.dot(rows, weight, preferred_element_type=jnp.float32).astype(jnp.bfloat16)

    cuts = [slice(0, width // 2), slice(width // 2, width)]
    state = []
    for r in range(requests):
        attended = attend(
            r,
            prefix_length,
            parity,
            queries,
            prefix_key_value_cache,
            incoming_key_value,
            arrived[r],
            arrived_new,
        )
        across = partner(attended, "dp", 0)
        flat = jnp.dot(attended, down, preferred_element_type=jnp.float32)
        rank = lax.dynamic_slice(
            flat, (0, adapter[r] * ADAPTER_RANK), (NEW, ADAPTER_RANK)
        ).astype(jnp.bfloat16)
        rank = jnp.pad(rank, ((0, 0), (0, HEAD_SIZE - ADAPTER_RANK)))
        payload = jnp.concatenate([product(attended, weight_send), rank], axis=1)
        got_mine = partner(payload, "tensor", 0)
        keep_mine = product(attended, weight_keep)
        sent_theirs = product(across, weight_send)
        sent_theirs = [sent_theirs[:, cut] for cut in cuts]
        if r + 1 < requests:
            keep_mine, arrived[r + 1], _ = lax.optimization_barrier(
                (keep_mine, arrived[r + 1], sent_theirs)
            )
        got_theirs = [partner(block, "tensor", 0) for block in sent_theirs]
        keep_theirs = product(across, weight_keep)
        keep_mine, keep_theirs = lax.optimization_barrier((keep_mine, keep_theirs))
        state.append((rank, keep_mine, keep_theirs, got_mine, got_theirs))

    def pair_sum(kept, got):
        return (kept.astype(jnp.float32) + got.astype(jnp.float32)).astype(jnp.bfloat16)

    hidden = []
    before = None
    for r in range(requests):
        rank, keep_mine, keep_theirs, got_mine, got_theirs = state[r]
        if before is not None:
            got_mine, got_theirs[0], _ = lax.optimization_barrier(
                (got_mine, got_theirs[0], (before[0], payload))
            )
            earlier = before[1]
        rank_pair = pair_sum(rank, got_mine[:, width:])
        kept, before = [], []
        for i, cut in enumerate(cuts):
            if i > 0:
                got_theirs[i], _ = lax.optimization_barrier((got_theirs[i], crossing))
            crossing = pair_sum(keep_theirs[:, cut], got_theirs[i])
            theirs = partner(crossing, "dp", 0)
            if i > 0:
                theirs, _ = lax.optimization_barrier((theirs, payload))
            elif r > 0:
                theirs, _ = lax.optimization_barrier((theirs, earlier))
            mine = pair_sum(keep_mine[:, cut], got_mine[:, cut])
            kept.append(jnp.where(x == upper, mine, theirs))
            payload = jnp.where(x == upper, theirs, mine)
            if i == 0:
                payload = jnp.concatenate([payload, rank_pair], axis=1)
            before.append(partner(payload, "tensor", 1))
        shrunk = pair_sum(rank_pair, before[0][:, width // 2 :])[:, :ADAPTER_RANK]
        up = lax.dynamic_slice(
            adapter_up_weight, (adapter[r], 0, 0), (1, ADAPTER_RANK, width)
        )[0]
        pieces = []
        for i, cut in enumerate(cuts):
            got = before[i][:, : width // 2].astype(jnp.float32)
            projected = kept[i].astype(jnp.float32) + got
            adapter_output = jnp.dot(shrunk, up[:, cut], preferred_element_type=jnp.float32)
            rows = residual[r * NEW : (r + 1) * NEW, cut].astype(jnp.float32)
            pieces.append((rows + projected + adapter_output).astype(jnp.bfloat16))
        hidden.append(jnp.concatenate(pieces, axis=1))
    hidden = jnp.concatenate(hidden, axis=0)
    widened = hidden.astype(jnp.float32)
    own_squares = jnp.sum(widened * widened, axis=1)
    squares = own_squares
    for piece in from_others(own_squares, "tensor"):
        squares = squares + piece
    inverse = lax.rsqrt(squares / MODEL_WIDTH + eps_norm)
    normed = (widened * inverse[:, None] * norm_scale_weight.astype(jnp.float32)[None, :]).astype(
        jnp.bfloat16
    )
    return (hidden, normed)


def solution(mesh):
    sizes = tuple(mesh.shape[name] for name in ("tensor", "dp", "pipe"))
    shards = shards_fast if sizes == (4, 2, 2) else shards_any
    return jax.shard_map(
        shards,
        mesh=mesh,
        in_specs=(
            P(("groups", "dp", "pipe"), "tensor"),
            P(("groups", "dp", "pipe"), "tensor"),
            P(("groups", "dp", "pipe"), None, "tensor"),
            P(("groups", "dp", "pipe")),
            P(("groups", "dp", "pipe")),
            P("tensor", ("dp", "pipe")),
            P("tensor", None, None),
            P(None, None, "tensor"),
            P(("groups", "dp", "pipe"), "tensor"),
            P("tensor"),
        ),
        out_specs=(P(("groups", "dp", "pipe"), "tensor"), P(("groups", "dp", "pipe"), "tensor")),
        check_vma=False,
    )
```
